32 devices in a mesh: groups: 2 (over y), page: 8 (over z, core), head: 2 (over x), sub: 1.
Axes of the slice: x: 2, y: 2, z: 4, core: 2. Of those that a mesh axis runs over, the one named last changes fastest.
Arguments:
- queries: bfloat16 [128, 3, 16384], P(('groups', 'page', 'sub'), None, 'head'), parts along dimension 0, may hold values from -400 to 400
- page_keys: bfloat16 [128, 128, 1024], P(('groups', 'page'), None, 'head'), parts along dimension 0, may hold values from -6 to 6
- page_values: bfloat16 [128, 128, 1024], P(('groups', 'page'), None, 'head'), parts along dimension 0, may hold values from -6 to 6
- page_count: int32 [128], P(('groups', 'page')), parts along dimension 0, may hold values from 1 to 128
- leaf_keys: bfloat16 [128, 128, 1024], P(('groups', 'page', 'sub'), None, 'head'), parts along dimension 0, may hold values from -6 to 6
- leaf_values: bfloat16 [128, 128, 1024], P(('groups', 'page', 'sub'), None, 'head'), parts along dimension 0, may hold values from -6 to 6
- leaf_count: int32 [128], P(('groups', 'page', 'sub')), parts along dimension 0, may hold values from 1 to 128
- new_keys: bfloat16 [128, 3, 1024], P(('groups', 'page', 'sub'), None, 'head'), parts along dimension 0, may hold values from -6 to 6
- new_values: bfloat16 [128, 3, 1024], P(('groups', 'page', 'sub'), None, 'head'), parts along dimension 0, may hold values from -6 to 6
- path_owner: int32 [128, 3], P(('groups', 'page', 'sub')), parts along dimension 0, may hold values from 0 to 7, all different within a row; in each aligned block of 8 rows (0 to 7, 8 to 15, ...) at most 6 rows name the same one
- path_slot: int32 [128, 3], P(('groups', 'page', 'sub')), parts along dimension 0, may hold values from 0 to 7
Outputs:
- attended: bfloat16 [128, 3, 16384], P(('groups', 'page', 'sub'), None, 'head'), parts along dimension 0
The draws below stay inside these ranges and needn't reach their ends.
There are 2 independent parts, one for each index of `groups`. The reference program is written for one: setup_inputs(seed, part) draws one part's arguments, and reference() takes and returns one part's arrays. A program takes and returns all parts, laid end to end along the dimension named above; each array names one. Nothing has to cross between parts.
Inputs may be any that keep to these rules, and one draw needn't show every extreme that they name: `path_owner`: each request names 3 different owners; the requests of one device (aligned blocks of 8 requests) name one owner at most 6 times.
All inputs are finite; a program needn't handle non-finite values.
Results may differ from the reference program's by a relative error of at most 0.0047.
Values may be sent and summed in bfloat16 or wider, within the bound.
No kernel may reach another device: no remote copies, remote signals or barrier semaphores. Data moves between devices by JAX's collectives and lax.ppermute only.
A program may use at most 64 MiB of HBM per device.

```python
import math
import jax
import jax.numpy as jnp
import numpy as np
from jax import lax

HD = 128
QH = 128
KVH = 8
GROUP = 16
PAGE_TOK = 128
STEPS = 3
LEVELS = 3
REQ_DEV = 8
PAGE_DEV = 8
REQ = 64
PAGES = 64
CAP = 6
N_PAGE = 8


def paired_keys(key, shape):
    normal_draw = jax.random.normal(key, shape, jnp.float32)
    return jnp.clip(normal_draw, -6.0, 6.0).astype(jnp.bfloat16)


def filled_counts(key, total):
    counts = jax.random.randint(jax.random.fold_in(key, 21), (total,), 1, PAGE_TOK + 1)
    spot = jax.random.randint(jax.random.fold_in(key, 22), (), 0, total)
    return counts.at[spot].set(PAGE_TOK).astype(jnp.int32)


def draw_queries(key, part):
    normal_draw = jax.random.normal(jax.random.fold_in(key, 303), (REQ, STEPS, QH * HD), jnp.float32)
    normal_draw = jnp.clip(normal_draw, -6.0, 6.0) * 2.0
    return jnp.clip(normal_draw, -400.0, 400.0).astype(jnp.bfloat16)


def draw_page_keys(key, part):
    return paired_keys(jax.random.fold_in(key, 101), (PAGES, PAGE_TOK, KVH * HD))


def draw_leaf_keys(key, part):
    return paired_keys(jax.random.fold_in(key, 202), (REQ, PAGE_TOK, KVH * HD))


def draw_page_count(key, part):
    return filled_counts(jax.random.fold_in(key, 405), PAGES)


def draw_leaf_count(key, part):
    return filled_counts(jax.random.fold_in(key, 506), REQ)


def place_ends(result, stream_key, least, top_value):
    shape = result.shape
    index_at = [jax.random.randint(jax.random.fold_in(stream_key, axis), (), 0, shape[axis]) for axis in range(len(shape))]
    result = result.at[tuple(index_at)].set(least)
    longest = shape.index(max(shape))
    index_at[longest] = (index_at[longest] + 1) % shape[longest]
    return result.at[tuple(index_at)].set(top_value)


def level_of(stream_key, dims, split, smallest, top_value):
    loudness = 1.0
    for axis_at, parts in split:
        steps = jax.random.uniform(jax.random.fold_in(jax.random.fold_in(stream_key, 6), axis_at), (parts,), jnp.float32, smallest / len(split), top_value / len(split))
        loudness = loudness * jnp.repeat(jnp.exp(steps), dims[axis_at] // parts).reshape((-1,) + (1,) * (len(dims) - 1 - axis_at))
    return loudness


def shared_out(rng, own, number, rows, amount, top, bound, skew):
    order = jax.random.permutation(rng, amount)
    crowded, usual = shares(amount, rows * top, bound, skew, True), shares(amount, rows * top, bound, skew, False)
    places = jnp.arange(amount)

    def named(sizes, rotation):
        used = int((sizes > 0).sum())
        fixed = max(1, used // 4)
        passed = fixed + (places - fixed + rotation * (used - fixed)) % max(1, amount - fixed)
        return jnp.zeros((amount,), jnp.int32).at[order[jnp.where(places < fixed, places, passed)]].set(jnp.asarray(sizes, jnp.int32))

    sizes = jnp.where(number % 4 == 0, named(crowded, number // 4), named(usual, number - number // 4 - 1))
    mixed = jax.random.permutation(jax.random.fold_in(own, 3), amount)
    giver, receiver = mixed[0:amount // 2 * 2:2], mixed[1:amount // 2 * 2:2]
    margin = jnp.minimum(sizes[giver] - 1, bound - sizes[receiver]) // 2
    margin = jnp.where((giver == order[0]) | (receiver == order[0]) | (sizes[receiver] == 0), 0, jnp.maximum(margin, 0))
    passed = jax.random.randint(jax.random.fold_in(own, 4), (amount // 2,), 0, 1 << 20) % (margin + 1)
    sizes = sizes.at[giver].add(-passed).at[receiver].add(passed)
    labels = jnp.searchsorted(jnp.cumsum(sizes), jnp.arange(rows * top), side="right").astype(jnp.int32)
    table = labels.reshape(top, rows).T
    table = table[jax.random.permutation(jax.random.fold_in(own, 1), rows)]
    rotation = jax.random.randint(jax.random.fold_in(own, 2), (rows, 1), 0, top)
    return jnp.take_along_axis(table, (jnp.arange(top)[None, :] + rotation) % top, axis=1)


def shares(number_of, total, reach, skew, full):
    weights = [(1 << 20) // math.isqrt(grade ** skew) + 1 for grade in range(1, number_of + 1)]
    largest = reach if full else min(reach, max(-(-total // number_of), total * weights[0] // sum(weights)))
    least = 1 if total - largest >= number_of - 1 else 0
    holding, surplus = [largest] + [least] * (number_of - 1), total - largest - least * (number_of - 1)
    while surplus > 0:
        free = [i for i in range(1, number_of) if holding[i] < largest] or [i for i in range(1, number_of) if holding[i] < reach]
        whole, remaining = sum([weights[i] for i in free]), surplus
        for i in free:
            more = min(reach - holding[i], max(1, remaining * weights[i] // whole), surplus)
            holding[i] = holding[i] + more
            surplus = surplus - more
    return np.array(holding)


def noise(own_key, dims, deviation, limit, shards=(), kind=jnp.bfloat16):
    loudness = level_of(own_key, dims, shards, -0.22, 0.18) if shards else 1.0
    values = jax.random.normal(own_key, dims, jnp.float32) * deviation * loudness
    return jnp.minimum(jnp.maximum(values, -limit), limit).astype(kind)


def setup_inputs(seed: int = 0, part: int = 0) -> dict:
    splits = jax.random.split(jax.random.key(seed), 12)
    own_keys = jax.random.split(jax.random.fold_in(splits[11], part), 12)
    queries = draw_queries(jax.random.fold_in(jax.random.fold_in(splits[11], part), 71), part)
    page_keys = draw_page_keys(jax.random.fold_in(jax.random.fold_in(splits[11], part), 71), part)
    page_values = noise(own_keys[2], (PAGES, PAGE_TOK, KVH * HD), 1.0, 6.0, ((0, 8), (2, 2)))
    page_count = draw_page_count(jax.random.fold_in(jax.random.fold_in(splits[11], part), 71), part)
    leaf_keys = draw_leaf_keys(jax.random.fold_in(jax.random.fold_in(splits[11], part), 71), part)
    leaf_values = noise(own_keys[5], (REQ, PAGE_TOK, KVH * HD), 1.0, 6.0, ((0, 8), (2, 2)))
    leaf_count = draw_leaf_count(jax.random.fold_in(jax.random.fold_in(splits[11], part), 71), part)
    new_keys = noise(own_keys[7], (REQ, STEPS, KVH * HD), 1.0, 6.0, ((0, 8), (2, 2)))
    new_values = noise(own_keys[8], (REQ, STEPS, KVH * HD), 1.0, 6.0, ((0, 8), (2, 2)))
    path_owner_keys = jax.random.split(jax.random.fold_in(own_keys[9], 1), REQ // REQ_DEV)
    path_owner_turns = jax.random.permutation(jax.random.fold_in(own_keys[9], 3), REQ // REQ_DEV)
    path_owner = jax.vmap(lambda own, number: shared_out(jax.random.fold_in(own_keys[9], 2), own, number, REQ_DEV, N_PAGE, LEVELS, CAP, 2))(path_owner_keys, path_owner_turns).reshape((REQ, LEVELS))
    path_slot = place_ends(jax.random.randint(own_keys[10], (REQ, LEVELS), 0, PAGE_DEV), jax.random.fold_in(own_keys[10], 1), 0, PAGE_DEV - 1).astype(jnp.int32)
    return {"queries": queries, "page_keys": page_keys, "page_values": page_values, "page_count": page_count, "leaf_keys": leaf_keys, "leaf_values": leaf_values, "leaf_count": leaf_count, "new_keys": new_keys, "new_values": new_values, "path_owner": path_owner, "path_slot": path_slot}


def settle(weights):
    return lax.optimization_barrier(weights.astype(jnp.bfloat16)).astype(jnp.float32)

def reference(queries, page_keys, page_values, page_count, leaf_keys, leaf_values, leaf_count, new_keys, new_values, path_owner, path_slot):
    score_scale = 1.0 / math.sqrt(HD)
    block_rows = REQ_DEV
    block_total = REQ // block_rows
    page_index = (path_owner * PAGE_DEV + path_slot).astype(jnp.int32)

    def shaped(array):
        return array.reshape((block_total, block_rows) + array.shape[1:])

    def per_block(packed):
        query_rows, leaf_key_rows, leaf_value_rows, leaf_length, fresh_keys, fresh_values, wanted = packed
        query_five = query_rows.astype(jnp.float32).reshape(block_rows, STEPS, KVH, GROUP, HD)
        page_key_rows = jnp.take(page_keys, wanted, axis=0).astype(jnp.float32).reshape(block_rows, LEVELS, PAGE_TOK, KVH, HD)
        page_value_rows = jnp.take(page_values, wanted, axis=0).astype(jnp.float32).reshape(block_rows, LEVELS, PAGE_TOK, KVH, HD)
        lengths = jnp.take(page_count, wanted, axis=0)
        token_pos = jnp.arange(PAGE_TOK, dtype=jnp.int32)
        scores = jnp.einsum('bskgd,bltkd->blskgt', query_five, page_key_rows) * score_scale
        allowed = (token_pos[None, None, :] < lengths[:, :, None])[:, :, None, None, None, :]
        scores = jnp.where(allowed, scores, -jnp.inf)
        item_max = lax.optimization_barrier(jnp.max(scores, axis=-1))
        weights = jnp.exp(scores - item_max[..., None])
        item_total = lax.optimization_barrier(jnp.sum(weights, axis=-1))
        item_out = jnp.einsum('blskgt,bltkd->blskgd', settle(weights), page_value_rows) / item_total[..., None]
        item_out = settle(item_out)
        leaf_five = leaf_key_rows.astype(jnp.float32).reshape(block_rows, PAGE_TOK, KVH, HD)
        leaf_vfive = leaf_value_rows.astype(jnp.float32).reshape(block_rows, PAGE_TOK, KVH, HD)
        fresh_five = fresh_keys.astype(jnp.float32).reshape(block_rows, STEPS, KVH, HD)
        fresh_vfive = fresh_values.astype(jnp.float32).reshape(block_rows, STEPS, KVH, HD)
        leaf_scores = jnp.einsum('bskgd,btkd->bskgt', query_five, leaf_five) * score_scale
        leaf_allowed = token_pos[None, :] < leaf_length[:, None]
        leaf_scores = jnp.where(leaf_allowed[:, None, None, None, :], leaf_scores, -jnp.inf)
        fresh_scores = jnp.einsum('bskgd,bukd->bskgu', query_five, fresh_five) * score_scale
        causal = jnp.arange(STEPS, dtype=jnp.int32)[None, :] <= jnp.arange(STEPS, dtype=jnp.int32)[:, None]
        fresh_scores = jnp.where(causal[None, :, None, None, :], fresh_scores, -jnp.inf)
        local_max = jnp.maximum(lax.optimization_barrier(jnp.max(leaf_scores, axis=-1)), lax.optimization_barrier(jnp.max(fresh_scores, axis=-1)))
        leaf_weights = jnp.exp(leaf_scores - local_max[..., None])
        fresh_weights = jnp.exp(fresh_scores - local_max[..., None])
        local_total = lax.optimization_barrier(jnp.sum(leaf_weights, axis=-1)) + lax.optimization_barrier(jnp.sum(fresh_weights, axis=-1))
        local_out = (jnp.einsum('bskgt,btkd->bskgd', settle(leaf_weights), leaf_vfive) + jnp.einsum('bskgu,bukd->bskgd', settle(fresh_weights), fresh_vfive)) / local_total[..., None]
        top_score = jnp.maximum(local_max, lax.optimization_barrier(jnp.max(item_max, axis=1)))
        local_mass = local_total * jnp.exp(local_max - top_score)
        item_mass = item_total * jnp.exp(item_max - top_score[:, None])
        numerator = local_mass[..., None] * local_out + lax.optimization_barrier(jnp.sum(item_mass[..., None] * item_out, axis=1))
        denominator = local_mass + lax.optimization_barrier(jnp.sum(item_mass, axis=1))
        return (numerator / denominator[..., None]).astype(jnp.bfloat16).reshape(block_rows, STEPS, QH * HD)
    outcome = lax.map(per_block, (shaped(queries), shaped(leaf_keys), shaped(leaf_values), shaped(leaf_count), shaped(new_keys), shaped(new_values), shaped(page_index)))
    return outcome.reshape(REQ, STEPS, QH * HD)
```

```python
import functools
import math

import jax
import jax.numpy as jnp
from jax import lax
from jax.experimental import pallas as pl
from jax.experimental.pallas import tpu as pltpu
from jax.sharding import PartitionSpec as P

HD = 128
QH = 128
KVH = 8


def page_states(query_rows, keys, values, counts):
    slot_rows = query_rows.shape[0]
    kv_local = keys.shape[2] // HD
    group_size = QH // KVH
    step_count = query_rows.shape[1] // (kv_local * group_size * HD)
    page_tok = keys.shape[1]
    query_five = query_rows.reshape(slot_rows, step_count, kv_local, group_size, HD)
    key_heads = keys.reshape(slot_rows, page_tok, kv_local, HD)
    value_heads = values.reshape(slot_rows, page_tok, kv_local, HD)
    scores = jnp.einsum(
        "nskgd,ntkd->nskgt", query_five, key_heads, preferred_element_type=jnp.float32
    ) * (1.0 / math.sqrt(HD))
    allowed = jnp.arange(page_tok, dtype=jnp.int32)[None, :] < counts[:, None]
    scores = jnp.where(allowed[:, None, None, None, :], scores, -jnp.inf)
    item_max = jnp.max(scores, axis=-1)
    weights = jnp.exp(scores - item_max[..., None])
    item_total = jnp.sum(weights, axis=-1)
    mixed = jnp.einsum(
        "nskgt,ntkd->nskgd",
        weights.astype(jnp.bfloat16),
        value_heads,
        preferred_element_type=jnp.float32,
    )
    item_out = (mixed / item_total[..., None]).astype(jnp.bfloat16)
    return (
        item_out.reshape(slot_rows, -1),
        item_max.reshape(slot_rows, -1),
        item_total.reshape(slot_rows, -1),
    )


def in_blocks(step_fn, arrays, rows_per_slot):
    owner_count = arrays[0].shape[0]
    slot_width = arrays[0].shape[1]
    wanted_slots = -(-512 // max(1, slot_width * rows_per_slot))
    divisors = [
        candidate
        for candidate in range(1, owner_count + 1)
        if owner_count % candidate == 0 and candidate >= wanted_slots
    ]
    merge_count = min(divisors)
    merged = tuple(
        (
            member.reshape(
                (owner_count // merge_count, merge_count * slot_width) + member.shape[2:]
            )
            for member in arrays
        )
    )
    results = lax.map(step_fn, merged)
    return tuple(
        (member.reshape((owner_count, slot_width) + member.shape[2:]) for member in results)
    )


def shards(
    queries,
    page_keys,
    page_values,
    page_count,
    leaf_keys,
    leaf_values,
    leaf_count,
    new_keys,
    new_values,
    path_owner,
    path_slot,
):
    request_rows, step_count, head_width = queries.shape
    kv_local = page_keys.shape[2] // HD
    group_size = QH // KVH
    page_tok = page_keys.shape[1]
    level_count = path_owner.shape[1]
    owner_count = lax.axis_size("page")
    capacity = max(
        2, min(request_rows, (2 * request_rows * level_count + owner_count - 1) // owner_count)
    )
    score_scale = 1.0 / math.sqrt(HD)
    rows_per_slot = step_count * kv_local * group_size
    item_count = request_rows * level_count
    slot_count = owner_count * capacity
    flat_owner = path_owner.reshape(item_count)
    flat_slot = path_slot.reshape(item_count)
    owner_hot = (flat_owner[:, None] == jnp.arange(owner_count, dtype=jnp.int32)[None, :]).astype(
        jnp.int32
    )
    earlier = jnp.cumsum(owner_hot, axis=0) - owner_hot
    owner_rank = jnp.sum(earlier * owner_hot, axis=1)
    position = flat_owner * capacity + owner_rank
    slot_match = (position[None, :] == jnp.arange(slot_count, dtype=jnp.int32)[:, None]).astype(
        jnp.int32
    )
    item_of_slot = jnp.sum(slot_match * jnp.arange(item_count, dtype=jnp.int32)[None, :], axis=1)
    slot_used = jnp.sum(slot_match, axis=1) > 0
    page_ids = jnp.where(slot_used, jnp.take(flat_slot, item_of_slot, axis=0), 0).reshape(
        owner_count, capacity
    )
    outgoing = jnp.take(queries, item_of_slot // level_count, axis=0).reshape(
        owner_count, capacity, step_count * head_width
    )

    def remote_block(packed):
        block_ids = packed[1]
        return page_states(
            packed[0],
            jnp.take(page_keys, block_ids, axis=0),
            jnp.take(page_values, block_ids, axis=0),
            jnp.take(page_count, block_ids, axis=0),
        )

    states = in_blocks(
        remote_block,
        (
            lax.all_to_all(outgoing, "page", split_axis=0, concat_axis=0, tiled=True),
            lax.all_to_all(page_ids, "page", split_axis=0, concat_axis=0, tiled=True),
        ),
        rows_per_slot,
    )
    out_back = lax.all_to_all(states[0], "page", split_axis=0, concat_axis=0, tiled=True)
    max_back = lax.all_to_all(states[1], "page", split_axis=0, concat_axis=0, tiled=True)
    total_back = lax.all_to_all(states[2], "page", split_axis=0, concat_axis=0, tiled=True)
    item_out = jnp.take(out_back.reshape(slot_count, step_count * head_width), position, axis=0)
    item_out = item_out.astype(jnp.float32).reshape(
        request_rows, level_count, step_count, kv_local, group_size, HD
    )
    item_max = jnp.take(max_back.reshape(slot_count, rows_per_slot), position, axis=0)
    item_max = item_max.reshape(request_rows, level_count, step_count, kv_local, group_size)
    item_total = jnp.take(total_back.reshape(slot_count, rows_per_slot), position, axis=0)
    item_total = item_total.reshape(request_rows, level_count, step_count, kv_local, group_size)
    query_five = queries.reshape(request_rows, step_count, kv_local, group_size, HD)
    leaf_heads = leaf_keys.reshape(request_rows, page_tok, kv_local, HD)
    leaf_value_heads = leaf_values.reshape(request_rows, page_tok, kv_local, HD)
    fresh_heads = new_keys.reshape(request_rows, step_count, kv_local, HD)
    fresh_value_heads = new_values.reshape(request_rows, step_count, kv_local, HD)
    leaf_scores = (
        jnp.einsum("rskgd,rtkd->rskgt", query_five, leaf_heads, preferred_element_type=jnp.float32)
        * score_scale
    )
    leaf_allowed = jnp.arange(page_tok, dtype=jnp.int32)[None, :] < leaf_count[:, None]
    leaf_scores = jnp.where(leaf_allowed[:, None, None, None, :], leaf_scores, -jnp.inf)
    fresh_scores = (
        jnp.einsum("rskgd,rukd->rskgu", query_five, fresh_heads, preferred_element_type=jnp.float32)
        * score_scale
    )
    causal = (
        jnp.arange(step_count, dtype=jnp.int32)[None, :]
        <= jnp.arange(step_count, dtype=jnp.int32)[:, None]
    )
    fresh_scores = jnp.where(causal[None, :, None, None, :], fresh_scores, -jnp.inf)
    local_max = jnp.maximum(jnp.max(leaf_scores, axis=-1), jnp.max(fresh_scores, axis=-1))
    leaf_weights = jnp.exp(leaf_scores - local_max[..., None])
    fresh_weights = jnp.exp(fresh_scores - local_max[..., None])
    local_total = jnp.sum(leaf_weights, axis=-1) + jnp.sum(fresh_weights, axis=-1)
    local_sum = jnp.einsum(
        "rskgt,rtkd->rskgd",
        leaf_weights.astype(jnp.bfloat16),
        leaf_value_heads,
        preferred_element_type=jnp.float32,
    )
    local_sum = local_sum + jnp.einsum(
        "rskgu,rukd->rskgd",
        fresh_weights.astype(jnp.bfloat16),
        fresh_value_heads,
        preferred_element_type=jnp.float32,
    )
    local_out = local_sum / local_total[..., None]
    top_score = jnp.maximum(local_max, jnp.max(item_max, axis=1))
    local_mass = local_total * jnp.exp(local_max - top_score)
    item_mass = item_total * jnp.exp(item_max - top_score[:, None])
    numerator = local_mass[..., None] * local_out + jnp.sum(item_mass[..., None] * item_out, axis=1)
    denominator = local_mass + jnp.sum(item_mass, axis=1)
    return (
        (numerator / denominator[..., None])
        .astype(jnp.bfloat16)
        .reshape(request_rows, step_count, head_width)
    )


NEG = -3e38
CORES = 2


def packed_stats(tile):
    return tile + pltpu.roll(tile, tile.shape[1] - 1, 1)


def put_lane(tile, lane_ids, lane, column):
    return jnp.where(lane_ids == lane, column, tile)


def two_pieces(column):
    high = column.astype(jnp.bfloat16).astype(jnp.float32)
    low = (column - high).astype(jnp.bfloat16).astype(jnp.float32)
    return high, low


def dot_nt(a, b):
    return lax.dot_general(a, b, (((1,), (1,)), ((), ())), preferred_element_type=jnp.float32)


def dot_nn(a, b):
    return lax.dot_general(a, b, (((1,), (0,)), ((), ())), preferred_element_type=jnp.float32)


def plain_call(kernel, out_shape, in_memory, scratch=(), flops=0, num_bytes=0, exps=0):
    return pl.pallas_call(
        kernel,
        out_shape=out_shape,
        in_specs=[pl.BlockSpec(memory_space=space) for space in in_memory],
        out_specs=jax.tree.map(lambda _: pl.BlockSpec(memory_space=pltpu.VMEM), out_shape),
        scratch_shapes=list(scratch),
        compiler_params=pltpu.CompilerParams(vmem_limit_bytes=32 * 1024 * 1024),
        cost_estimate=pl.CostEstimate(flops=flops, bytes_accessed=num_bytes, transcendentals=exps),
    )


class Sizes:
    def __init__(self, requests, steps, kv, group, levels, pages, page_tok, owners):
        self.requests, self.steps, self.kv, self.group = requests, steps, kv, group
        self.levels, self.pages, self.page_tok, self.owners = levels, pages, page_tok, owners
        self.rows = steps * group
        self.step_rows = kv * group
        self.all_rows = requests * steps * kv * group
        self.tile_count = -(-requests * kv * 4 // HD)
        self.stat_rows = self.tile_count * self.rows
        self.table = pages + 2 * requests * levels
        self.scale = 1.0 / math.sqrt(HD)

    def head_rows(self, ref, request, head):
        base = request * (self.steps * self.step_rows) + head * self.group
        return jnp.concatenate(
            [ref[pl.ds(base + step * self.step_rows, self.group), :] for step in range(self.steps)],
            axis=0,
        )

    def put_rows(self, ref, request, head, value):
        base = request * (self.steps * self.step_rows) + head * self.group
        for step in range(self.steps):
            ref[pl.ds(base + step * self.step_rows, self.group), :] = value[
                step * self.group : (step + 1) * self.group
            ].astype(ref.dtype)

    def find(self, table_ref, source, owner, request):
        base = source * self.table + self.pages + request * self.levels
        slot = jnp.int32(0)
        used = jnp.int32(0)
        for level in range(self.levels):
            hit = table_ref[base + level] == owner
            slot = jnp.where(hit, table_ref[base + self.requests * self.levels + level], slot)
            used = jnp.where(hit, 1, used)
        return slot, used * table_ref[owner * self.table + slot]


def shared_kernel(sz, hop, exact, table_ref, q_ref, k0, v0, k1, v1, *outs):
    num_ref, stat_ref = outs if exact else (outs[0], None)
    me = lax.axis_index("page")
    source = jnp.bitwise_xor(me, hop)
    mate = jnp.bitwise_xor(me, 1)
    lane_ids = lax.broadcasted_iota(jnp.int32, (sz.rows, HD), 1)
    token_ids = lax.broadcasted_iota(jnp.int32, (sz.rows, sz.page_tok), 1)
    per_tile = HD // (4 * sz.kv)
    empty = jnp.where(lane_ids % 4 == 0, NEG, 0.0).astype(jnp.bfloat16).astype(jnp.float32)
    for tile_at in range(sz.tile_count):

        def one(request, tile):
            slot0, count0 = sz.find(table_ref, source, me, request)
            slot1, count1 = sz.find(table_ref, source, mate, request)

            def work(tile):
                for head in range(sz.kv):
                    cols = slice(head * HD, (head + 1) * HD)
                    q = sz.head_rows(q_ref, request, head)
                    s0 = dot_nt(q, k0[slot0, :, cols]) * sz.scale
                    s1 = dot_nt(q, k1[slot1, :, cols]) * sz.scale
                    s0 = jnp.where(token_ids < count0, s0, NEG)
                    s1 = jnp.where(token_ids < count1, s1, NEG)
                    top = jnp.max(jnp.maximum(s0, s1), axis=1, keepdims=True)
                    high, low = two_pieces(top)
                    point = high + low
                    w0 = jnp.exp(s0 - point)
                    w1 = jnp.exp(s1 - point)
                    total = jnp.sum(w0 + w1, axis=1, keepdims=True)
                    num = dot_nn(w0.astype(jnp.bfloat16), v0[slot0, :, cols]) + dot_nn(
                        w1.astype(jnp.bfloat16), v1[slot1, :, cols]
                    )
                    sz.put_rows(num_ref, request, head, num)
                    total_high, total_low = two_pieces(total)
                    lane = ((request - tile_at * per_tile) * sz.kv + head) * 4
                    for piece_at, piece in enumerate((high, low, total_high, total_low)):
                        tile = put_lane(tile, lane_ids, lane + piece_at, piece)
                return tile

            def skip(tile):
                for head in range(sz.kv):
                    sz.put_rows(num_ref, request, head, jnp.zeros((sz.rows, HD), jnp.float32))
                return tile

            return lax.cond(count0 + count1 > 0, work, skip, tile)

        last = min(sz.requests, (tile_at + 1) * per_tile)
        tile = lax.fori_loop(tile_at * per_tile, last, one, empty)
        span = pl.ds(tile_at * sz.rows, sz.rows)
        if exact:
            stat_ref[span, :] = tile
        else:
            num_ref[pl.ds(sz.all_rows + tile_at * sz.rows, sz.rows), :] = tile.astype(jnp.bfloat16)


def local_kernel(
    sz, table_ref, leaf_count_ref, q_ref, k0, v0, k1, v1, leaf_k, leaf_v, new_k, new_v, num_ref, stat_ref
):
    me = lax.axis_index("page")
    mate = jnp.bitwise_xor(me, 1)
    lane_ids = lax.broadcasted_iota(jnp.int32, (sz.rows, HD), 1)
    token_ids = lax.broadcasted_iota(jnp.int32, (sz.rows, sz.page_tok), 1)
    fresh = new_k.shape[0]
    fresh_ids = lax.broadcasted_iota(jnp.int32, (sz.rows, fresh), 1)
    step_ids = lax.broadcasted_iota(jnp.int32, (sz.rows, fresh), 0) // sz.group
    per_tile = HD // (4 * sz.kv)
    for tile_at in range(sz.tile_count):

        def one(request, tile):
            slot0, count0 = sz.find(table_ref, me, me, request)
            slot1, count1 = sz.find(table_ref, me, mate, request)
            count2 = leaf_count_ref[request]
            first = request * sz.steps
            for head in range(sz.kv):
                cols = slice(head * HD, (head + 1) * HD)
                q = sz.head_rows(q_ref, request, head)
                keys = (k0[slot0, :, cols], k1[slot1, :, cols], leaf_k[request, :, cols])
                values = (
                    v0[slot0, :, cols],
                    v1[slot1, :, cols],
                    leaf_v[request, :, cols],
                    new_v[:, cols],
                )
                scores = [
                    jnp.where(token_ids < count, dot_nt(q, key) * sz.scale, NEG)
                    for key, count in zip(keys, (count0, count1, count2))
                ]
                allowed = (fresh_ids >= first) & (fresh_ids <= first + step_ids)
                scores.append(jnp.where(allowed, dot_nt(q, new_k[:, cols]) * sz.scale, NEG))
                top = jnp.maximum(scores[0], scores[1])
                top = jnp.max(jnp.maximum(top, scores[2]), axis=1, keepdims=True)
                top = jnp.maximum(top, jnp.max(scores[3], axis=1, keepdims=True))
                weights = [jnp.exp(score - top) for score in scores]
                total = jnp.sum(weights[0] + weights[1] + weights[2], axis=1, keepdims=True)
                total = total + jnp.sum(weights[3], axis=1, keepdims=True)
                num = sum(
                    dot_nn(weight.astype(jnp.bfloat16), value)
                    for weight, value in zip(weights, values)
                )
                sz.put_rows(num_ref, request, head, num)
                lane = ((request - tile_at * per_tile) * sz.kv + head) * 4
                tile = put_lane(tile, lane_ids, lane, top)
                tile = put_lane(tile, lane_ids, lane + 2, total)
            return tile

        last = min(sz.requests, (tile_at + 1) * per_tile)
        tile = lax.fori_loop(
            tile_at * per_tile, last, one, jnp.zeros((sz.rows, HD), jnp.float32)
        )
        stat_ref[pl.ds(tile_at * sz.rows, sz.rows), :] = tile


def merge_kernel(sz, num_ref, stat_ref, came_ref, out_ref):
    lane_ids = lax.broadcasted_iota(jnp.int32, (sz.rows, HD), 1)
    per_tile = HD // (4 * sz.kv)
    for tile_at in range(sz.tile_count):
        span = pl.ds(tile_at * sz.rows, sz.rows)
        came_span = pl.ds(sz.all_rows + tile_at * sz.rows, sz.rows)
        mine = packed_stats(stat_ref[span, :])
        came = packed_stats(came_ref[came_span, :].astype(jnp.float32))
        top = jnp.maximum(mine, came)
        keep, add = jnp.exp(mine - top), jnp.exp(came - top)
        total = mine * pltpu.roll(keep, 2, 1) + came * pltpu.roll(add, 2, 1)
        high, low = two_pieces(top)
        total_high, total_low = two_pieces(total)
        kind = lane_ids % 4
        tile = jnp.where(kind == 0, high, pltpu.roll(low, 1, 1))
        tile = jnp.where(kind == 2, total_high, tile)
        tile = jnp.where(kind == 3, pltpu.roll(total_low, 1, 1), tile)
        out_ref[came_span, :] = tile.astype(jnp.bfloat16)
        for request in range(tile_at * per_tile, min(sz.requests, (tile_at + 1) * per_tile)):
            for head in range(sz.kv):
                lane = ((request - tile_at * per_tile) * sz.kv + head) * 4
                joined = sz.head_rows(num_ref, request, head) * keep[:, lane : lane + 1]
                joined = joined + (
                    sz.head_rows(came_ref, request, head).astype(jnp.float32)
                    * add[:, lane : lane + 1]
                )
                sz.put_rows(out_ref, request, head, joined)


def final_kernel(sz, num_ref, stat_ref, near_ref, far_ref, out_ref):
    per_tile = HD // (4 * sz.kv)
    for tile_at in range(sz.tile_count):
        span = pl.ds(tile_at * sz.rows, sz.rows)
        came_span = pl.ds(sz.all_rows + tile_at * sz.rows, sz.rows)
        mine = stat_ref[span, :]
        near = packed_stats(near_ref[came_span, :].astype(jnp.float32))
        far = packed_stats(far_ref[came_span, :].astype(jnp.float32))
        top = jnp.maximum(jnp.maximum(mine, near), far)
        parts = [jnp.exp(one - top) for one in (mine, near, far)]
        total = sum(
            one * pltpu.roll(part, 2, 1) for one, part in zip((mine, near, far), parts)
        )
        total = pltpu.roll(total, HD - 2, 1)
        parts = [part / total for part in parts]
        for request in range(tile_at * per_tile, min(sz.requests, (tile_at + 1) * per_tile)):
            for head in range(sz.kv):
                lane = ((request - tile_at * per_tile) * sz.kv + head) * 4
                joined = sum(
                    sz.head_rows(ref, request, head).astype(jnp.float32) * part[:, lane : lane + 1]
                    for ref, part in zip((num_ref, near_ref, far_ref), parts)
                )
                sz.put_rows(out_ref, request, head, joined)


def line_shards(
    queries,
    page_keys,
    page_values,
    page_count,
    leaf_keys,
    leaf_values,
    leaf_count,
    new_keys,
    new_values,
    path_owner,
    path_slot,
):
    requests, steps, width = queries.shape
    owners = lax.axis_size("page")
    sz = Sizes(
        requests,
        steps,
        page_keys.shape[2] // HD,
        QH // KVH,
        path_owner.shape[1],
        page_keys.shape[0],
        page_keys.shape[1],
        owners,
    )

    def exchange(array, hop):
        return lax.ppermute(array, "page", [(at, at ^ hop) for at in range(owners)])

    near, far = CORES, owners - CORES
    table = jnp.concatenate([page_count, path_owner.reshape(-1), path_slot.reshape(-1)])
    table = lax.all_gather(table, "page", tiled=True)
    block = queries.reshape(sz.all_rows, HD)
    far_q = exchange(block, far)
    near_q = exchange(block, near)
    mate_keys = exchange(page_keys, 1)
    mate_values = exchange(page_values, 1)

    smem, vmem = pltpu.SMEM, pltpu.VMEM
    sent = jax.ShapeDtypeStruct((sz.all_rows + sz.stat_rows, HD), jnp.bfloat16)
    exact = (
        jax.ShapeDtypeStruct((sz.all_rows, HD), jnp.float32),
        jax.ShapeDtypeStruct((sz.stat_rows, HD), jnp.float32),
    )
    pages = (page_keys, page_values, mate_keys, mate_values)
    flops = sz.all_rows * HD * sz.page_tok * 8
    page_bytes = 4 * page_keys.size * 2 + sz.all_rows * HD * 4

    def shared(hop, is_exact, block):
        return plain_call(
            functools.partial(shared_kernel, sz, hop, is_exact),
            exact if is_exact else (sent,),
            [smem] + [vmem] * 5,
            flops=flops,
            num_bytes=page_bytes,
        )(table, block, *pages)

    fresh_rows = -(-requests * steps // HD) * HD
    pad = ((0, fresh_rows - requests * steps), (0, 0))
    fresh_keys = jnp.pad(new_keys.reshape(requests * steps, -1), pad)
    fresh_values = jnp.pad(new_values.reshape(requests * steps, -1), pad)
    local_num, local_stat = plain_call(
        functools.partial(local_kernel, sz),
        exact,
        [smem, smem] + [vmem] * 9,
        flops=flops * 2,
        num_bytes=page_bytes * 2,
    )(table, leaf_count, block, *pages, leaf_keys, leaf_values, fresh_keys, fresh_values)
    (near_part,) = shared(near, False, near_q)
    far_num, far_stat = shared(far, True, far_q)
    cross_q = exchange(far_q, near)
    (cross_part,) = shared(near ^ far, False, cross_q)
    cross_back = exchange(cross_part, near)
    (far_part,) = plain_call(
        functools.partial(merge_kernel, sz), (sent,), [vmem] * 3, num_bytes=sz.all_rows * HD * 8
    )(far_num, far_stat, cross_back)
    far_back = exchange(far_part, far)
    near_back = exchange(near_part, near)
    (out,) = plain_call(
        functools.partial(final_kernel, sz),
        (jax.ShapeDtypeStruct((sz.all_rows, HD), jnp.bfloat16),),
        [vmem] * 4,
        num_bytes=sz.all_rows * HD * 10,
    )(local_num, local_stat, near_back, far_back)
    return out.reshape(requests, steps, width)


def solution(mesh):
    on_line = mesh.shape["sub"] == 1 and mesh.shape["page"] == 4 * CORES
    return jax.shard_map(
        line_shards if on_line else shards,
        mesh=mesh,
        in_specs=(
            P(("groups", "page", "sub"), None, "head"),
            P(("groups", "page"), None, "head"),
            P(("groups", "page"), None, "head"),
            P(("groups", "page")),
            P(("groups", "page", "sub"), None, "head"),
            P(("groups", "page", "sub"), None, "head"),
            P(("groups", "page", "sub")),
            P(("groups", "page", "sub"), None, "head"),
            P(("groups", "page", "sub"), None, "head"),
            P(("groups", "page", "sub"), None),
            P(("groups", "page", "sub"), None),
        ),
        out_specs=P(("groups", "page", "sub"), None, "head"),
        check_vma=False,
    )
```

```python
import functools
import math

import jax
import jax.numpy as jnp
from jax import lax
from jax.experimental import pallas as pl
from jax.experimental.pallas import tpu as pltpu
from jax.sharding import PartitionSpec as P

HD = 128
QH = 128
KVH = 8


def page_states(query_rows, keys, values, counts):
    slot_rows = query_rows.shape[0]
    kv_local = keys.shape[2] // HD
    group_size = QH // KVH
    step_count = query_rows.shape[1] // (kv_local * group_size * HD)
    page_tok = keys.shape[1]
    query_five = query_rows.reshape(slot_rows, step_count, kv_local, group_size, HD)
    key_heads = keys.reshape(slot_rows, page_tok, kv_local, HD)
    value_heads = values.reshape(slot_rows, page_tok, kv_local, HD)
    scores = jnp.einsum(
        "nskgd,ntkd->nskgt", query_five, key_heads, preferred_element_type=jnp.float32
    ) * (1.0 / math.sqrt(HD))
    allowed = jnp.arange(page_tok, dtype=jnp.int32)[None, :] < counts[:, None]
    scores = jnp.where(allowed[:, None, None, None, :], scores, -jnp.inf)
    item_max = jnp.max(scores, axis=-1)
    weights = jnp.exp(scores - item_max[..., None])
    item_total = jnp.sum(weights, axis=-1)
    mixed = jnp.einsum(
        "nskgt,ntkd->nskgd",
        weights.astype(jnp.bfloat16),
        value_heads,
        preferred_element_type=jnp.float32,
    )
    item_out = (mixed / item_total[..., None]).astype(jnp.bfloat16)
    return (
        item_out.reshape(slot_rows, -1),
        item_max.reshape(slot_rows, -1),
        item_total.reshape(slot_rows, -1),
    )


def in_blocks(step_fn, arrays, rows_per_slot):
    owner_count = arrays[0].shape[0]
    slot_width = arrays[0].shape[1]
    wanted_slots = -(-512 // max(1, slot_width * rows_per_slot))
    divisors = [
        candidate
        for candidate in range(1, owner_count + 1)
        if owner_count % candidate == 0 and candidate >= wanted_slots
    ]
    merge_count = min(divisors)
    merged = tuple(
        (
            member.reshape(
                (owner_count // merge_count, merge_count * slot_width) + member.shape[2:]
            )
            for member in arrays
        )
    )
    results = lax.map(step_fn, merged)
    return tuple(
        (member.reshape((owner_count, slot_width) + member.shape[2:]) for member in results)
    )


def shards(
    queries,
    page_keys,
    page_values,
    page_count,
    leaf_keys,
    leaf_values,
    leaf_count,
    new_keys,
    new_values,
    path_owner,
    path_slot,
):
    request_rows, step_count, head_width = queries.shape
    kv_local = page_keys.shape[2] // HD
    group_size = QH // KVH
    page_tok = page_keys.shape[1]
    level_count = path_owner.shape[1]
    owner_count = lax.axis_size("page")
    capacity = max(
        2, min(request_rows, (2 * request_rows * level_count + owner_count - 1) // owner_count)
    )
    score_scale = 1.0 / math.sqrt(HD)
    rows_per_slot = step_count * kv_local * group_size
    item_count = request_rows * level_count
    slot_count = owner_count * capacity
    flat_owner = path_owner.reshape(item_count)
    flat_slot = path_slot.reshape(item_count)
    owner_hot = (flat_owner[:, None] == jnp.arange(owner_count, dtype=jnp.int32)[None, :]).astype(
        jnp.int32
    )
    earlier = jnp.cumsum(owner_hot, axis=0) - owner_hot
    owner_rank = jnp.sum(earlier * owner_hot, axis=1)
    position = flat_owner * capacity + owner_rank
    slot_match = (position[None, :] == jnp.arange(slot_count, dtype=jnp.int32)[:, None]).astype(
        jnp.int32
    )
    item_of_slot = jnp.sum(slot_match * jnp.arange(item_count, dtype=jnp.int32)[None, :], axis=1)
    slot_used = jnp.sum(slot_match, axis=1) > 0
    page_ids = jnp.where(slot_used, jnp.take(flat_slot, item_of_slot, axis=0), 0).reshape(
        owner_count, capacity
    )
    outgoing = jnp.take(queries, item_of_slot // level_count, axis=0).reshape(
        owner_count, capacity, step_count * head_width
    )

    def remote_block(packed):
        block_ids = packed[1]
        return page_states(
            packed[0],
            jnp.take(page_keys, block_ids, axis=0),
            jnp.take(page_values, block_ids, axis=0),
            jnp.take(page_count, block_ids, axis=0),
        )

    states = in_blocks(
        remote_block,
        (
            lax.all_to_all(outgoing, "page", split_axis=0, concat_axis=0, tiled=True),
            lax.all_to_all(page_ids, "page", split_axis=0, concat_axis=0, tiled=True),
        ),
        rows_per_slot,
    )
    out_back = lax.all_to_all(states[0], "page", split_axis=0, concat_axis=0, tiled=True)
    max_back = lax.all_to_all(states[1], "page", split_axis=0, concat_axis=0, tiled=True)
    total_back = lax.all_to_all(states[2], "page", split_axis=0, concat_axis=0, tiled=True)
    item_out = jnp.take(out_back.reshape(slot_count, step_count * head_width), position, axis=0)
    item_out = item_out.astype(jnp.float32).reshape(
        request_rows, level_count, step_count, kv_local, group_size, HD
    )
    item_max = jnp.take(max_back.reshape(slot_count, rows_per_slot), position, axis=0)
    item_max = item_max.reshape(request_rows, level_count, step_count, kv_local, group_size)
    item_total = jnp.take(total_back.reshape(slot_count, rows_per_slot), position, axis=0)
    item_total = item_total.reshape(request_rows, level_count, step_count, kv_local, group_size)
    query_five = queries.reshape(request_rows, step_count, kv_local, group_size, HD)
    leaf_heads = leaf_keys.reshape(request_rows, page_tok, kv_local, HD)
    leaf_value_heads = leaf_values.reshape(request_rows, page_tok, kv_local, HD)
    fresh_heads = new_keys.reshape(request_rows, step_count, kv_local, HD)
    fresh_value_heads = new_values.reshape(request_rows, step_count, kv_local, HD)
    leaf_scores = (
        jnp.einsum("rskgd,rtkd->rskgt", query_five, leaf_heads, preferred_element_type=jnp.float32)
        * score_scale
    )
    leaf_allowed = jnp.arange(page_tok, dtype=jnp.int32)[None, :] < leaf_count[:, None]
    leaf_scores = jnp.where(leaf_allowed[:, None, None, None, :], leaf_scores, -jnp.inf)
    fresh_scores = (
        jnp.einsum("rskgd,rukd->rskgu", query_five, fresh_heads, preferred_element_type=jnp.float32)
        * score_scale
    )
    causal = (
        jnp.arange(step_count, dtype=jnp.int32)[None, :]
        <= jnp.arange(step_count, dtype=jnp.int32)[:, None]
    )
    fresh_scores = jnp.where(causal[None, :, None, None, :], fresh_scores, -jnp.inf)
    local_max = jnp.maximum(jnp.max(leaf_scores, axis=-1), jnp.max(fresh_scores, axis=-1))
    leaf_weights = jnp.exp(leaf_scores - local_max[..., None])
    fresh_weights = jnp.exp(fresh_scores - local_max[..., None])
    local_total = jnp.sum(leaf_weights, axis=-1) + jnp.sum(fresh_weights, axis=-1)
    local_sum = jnp.einsum(
        "rskgt,rtkd->rskgd",
        leaf_weights.astype(jnp.bfloat16),
        leaf_value_heads,
        preferred_element_type=jnp.float32,
    )
    local_sum = local_sum + jnp.einsum(
        "rskgu,rukd->rskgd",
        fresh_weights.astype(jnp.bfloat16),
        fresh_value_heads,
        preferred_element_type=jnp.float32,
    )
    local_out = local_sum / local_total[..., None]
    top_score = jnp.maximum(local_max, jnp.max(item_max, axis=1))
    local_mass = local_total * jnp.exp(local_max - top_score)
    item_mass = item_total * jnp.exp(item_max - top_score[:, None])
    numerator = local_mass[..., None] * local_out + jnp.sum(item_mass[..., None] * item_out, axis=1)
    denominator = local_mass + jnp.sum(item_mass, axis=1)
    return (
        (numerator / denominator[..., None])
        .astype(jnp.bfloat16)
        .reshape(request_rows, step_count, head_width)
    )


NEG = -3e38
CORES = 2


def pair_sums(tile):
    return tile + pltpu.roll(tile, tile.shape[1] - 1, 1)


def two_pieces(values):
    high = values.astype(jnp.bfloat16).astype(jnp.float32)
    low = (values - high).astype(jnp.bfloat16).astype(jnp.float32)
    return high, low


def dot_nt(a, b):
    return lax.dot_general(a, b, (((1,), (1,)), ((), ())), preferred_element_type=jnp.float32)


def dot_nn(a, b):
    return lax.dot_general(a, b, (((1,), (0,)), ((), ())), preferred_element_type=jnp.float32)


def plain_call(kernel, out_shape, in_memory, scratch=(), flops=0, num_bytes=0):
    return pl.pallas_call(
        kernel,
        out_shape=out_shape,
        in_specs=[pl.BlockSpec(memory_space=space) for space in in_memory],
        out_specs=tuple(pl.BlockSpec(memory_space=pltpu.VMEM) for _ in out_shape),
        scratch_shapes=list(scratch),
        compiler_params=pltpu.CompilerParams(vmem_limit_bytes=32 * 1024 * 1024),
        cost_estimate=pl.CostEstimate(flops=flops, bytes_accessed=num_bytes, transcendentals=0),
    )


class Sizes:
    def __init__(self, requests, steps, kv, group, levels, pages, page_tok):
        self.requests, self.steps, self.kv, self.group = requests, steps, kv, group
        self.levels, self.pages, self.page_tok = levels, pages, page_tok
        self.rows = steps * group
        self.step_rows = kv * group
        self.all_rows = requests * kv * self.rows
        self.per_tile = HD // (4 * kv)
        self.tile_count = -(-requests // self.per_tile)
        self.stat_rows = self.tile_count * self.rows
        self.factor = 1.0 / math.sqrt(HD) * math.log2(math.e)

    def tiles(self):
        for tile_at in range(self.tile_count):
            first = tile_at * self.per_tile
            yield tile_at, first, min(self.requests, first + self.per_tile)

    def read_table(self, q_ref, table_words, table_ref, sem):
        table_words[...] = q_ref[0, :, self.step_rows * HD :].astype(jnp.float32).astype(jnp.int32)
        copy = pltpu.make_async_copy(table_words, table_ref, sem)
        copy.start()
        return copy

    def spread(self, q_ref, wide):
        for step in range(self.steps):
            for head in range(self.step_rows):
                at = (step * self.step_rows + head) * self.requests
                wide[at : at + self.requests, :] = q_ref[
                    step, :, head * HD : (head + 1) * HD
                ].astype(jnp.float32)

    def pick(self, wide, request, kv_head):
        parts = []
        for step in range(self.steps):
            at = (step * self.step_rows + kv_head * self.group) * self.requests
            parts.append(wide[pl.ds(at + request, self.group, stride=self.requests), :])
        return jnp.concatenate(parts, axis=0)

    def span(self, request, kv_head):
        return pl.ds(pl.multiple_of((request * self.kv + kv_head) * self.rows, 16), self.rows)

    def find(self, table_ref, owner, request):
        slot, used = jnp.int32(0), jnp.int32(0)
        for level in range(self.levels):
            hit = table_ref[request, level] == owner
            slot = jnp.where(hit, table_ref[request, self.levels + level], slot)
            used = jnp.where(hit, 1, used)
        return slot, used


def shared_kernel(
    sz, exact, count0_ref, count1_ref, q_ref, k0, v0, k1, v1, *rest
):
    *outs, wide, table_words, table_ref, sem = rest
    num_ref = outs[0]
    me = lax.axis_index("page")
    mate = jnp.bitwise_xor(me, 1)
    lane_ids = lax.broadcasted_iota(jnp.int32, (sz.rows, HD), 1)
    token_ids = lax.broadcasted_iota(jnp.int32, (sz.rows, sz.page_tok), 1)
    heads = range(sz.kv)
    copy = sz.read_table(q_ref, table_words, table_ref, sem)
    sz.spread(q_ref, wide)
    copy.wait()
    for tile_at, first, last in sz.tiles():

        def one(request, tile):
            slot0, used0 = sz.find(table_ref, me, request)
            slot1, used1 = sz.find(table_ref, mate, request)
            allowed0 = token_ids < used0 * count0_ref[slot0]
            allowed1 = token_ids < used1 * count1_ref[slot1]

            def work(tile):
                cols = [slice(head * HD, (head + 1) * HD) for head in heads]
                q = [sz.pick(wide, request, head).astype(jnp.bfloat16) for head in heads]
                s0 = [dot_nt(q[h], k0[slot0, :, cols[h]]) for h in heads]
                s1 = [dot_nt(q[h], k1[slot1, :, cols[h]]) for h in heads]
                s0 = [jnp.where(allowed0, s, NEG) for s in s0]
                s1 = [jnp.where(allowed1, s, NEG) for s in s1]
                top = [jnp.max(jnp.maximum(a, b), axis=1, keepdims=True) for a, b in zip(s0, s1)]
                point = [sum(two_pieces(t)) for t in top]
                w0 = [jnp.exp2((s - p) * sz.factor) for s, p in zip(s0, point)]
                w1 = [jnp.exp2((s - p) * sz.factor) for s, p in zip(s1, point)]
                total = [jnp.sum(a + b, axis=1, keepdims=True) for a, b in zip(w0, w1)]
                num = [
                    dot_nn(w0[h].astype(jnp.bfloat16), v0[slot0, :, cols[h]])
                    + dot_nn(w1[h].astype(jnp.bfloat16), v1[slot1, :, cols[h]])
                    for h in heads
                ]
                for h in heads:
                    num_ref[sz.span(request, h), :] = num[h].astype(num_ref.dtype)
                    lane = ((request - first) * sz.kv + h) * 4
                    tile = jnp.where(lane_ids == lane, point[h], tile)
                    tile = jnp.where(lane_ids == lane + 2, total[h], tile)
                return tile

            def skip(tile):
                for h in heads:
                    num_ref[sz.span(request, h), :] = jnp.zeros((sz.rows, HD), num_ref.dtype)
                return tile

            return lax.cond(used0 + used1 > 0, work, skip, tile)

        empty = jnp.where(lane_ids % 4 == 0, NEG, 0.0)
        tile = lax.fori_loop(first, last, one, empty)
        if exact:
            outs[1][pl.ds(tile_at * sz.rows, sz.rows), :] = tile
        else:
            put_stats(sz, num_ref, tile_at, tile)


def put_stats(sz, out_ref, tile_at, tile):
    kind = lax.broadcasted_iota(jnp.int32, tile.shape, 1) % 4
    high, low = two_pieces(tile)
    tile = jnp.where(kind % 2 == 0, high, pltpu.roll(low, 1, 1))
    out_ref[pl.ds(sz.all_rows + tile_at * sz.rows, sz.rows), :] = tile.astype(jnp.bfloat16)


def local_kernel(
    sz,
    count0_ref,
    count1_ref,
    leaf_count_ref,
    q_ref,
    k0,
    v0,
    k1,
    v1,
    leaf_k,
    leaf_v,
    new_k,
    new_v,
    num_ref,
    stat_ref,
    wide,
    table_words,
    table_ref,
    sem,
    fresh_k,
    fresh_v,
):
    me = lax.axis_index("page")
    mate = jnp.bitwise_xor(me, 1)
    lane_ids = lax.broadcasted_iota(jnp.int32, (sz.rows, HD), 1)
    token_ids = lax.broadcasted_iota(jnp.int32, (sz.rows, sz.page_tok), 1)
    fresh = fresh_k.shape[0]
    fresh_ids = lax.broadcasted_iota(jnp.int32, (sz.rows, fresh), 1)
    step_ids = lax.broadcasted_iota(jnp.int32, (sz.rows, fresh), 0) // sz.group
    causal = (fresh_ids // sz.requests) <= step_ids
    fresh_request = fresh_ids % sz.requests
    heads = range(sz.kv)
    cols = [slice(head * HD, (head + 1) * HD) for head in heads]
    copy = sz.read_table(q_ref, table_words, table_ref, sem)
    sz.spread(q_ref, wide)
    copy.wait()
    for new_ref, full in ((new_k, fresh_k), (new_v, fresh_v)):
        rows = [new_ref[step].astype(jnp.float32) for step in range(sz.steps)]
        filler = fresh - sz.steps * sz.requests
        if filler:
            rows.append(jnp.zeros((filler, sz.kv * HD), jnp.float32))
        full[...] = jnp.concatenate(rows, axis=0).astype(full.dtype)
    for tile_at, first, last in sz.tiles():

        def one(request, tile):
            slot0, used0 = sz.find(table_ref, me, request)
            slot1, used1 = sz.find(table_ref, mate, request)
            allowed = (
                token_ids < used0 * count0_ref[slot0],
                token_ids < used1 * count1_ref[slot1],
                token_ids < leaf_count_ref[request],
                causal & (fresh_request == request),
            )
            places = ((k0, v0, slot0), (k1, v1, slot1), (leaf_k, leaf_v, request))
            q = [sz.pick(wide, request, head).astype(jnp.bfloat16) for head in heads]
            scores = []
            for h in heads:
                mine = [dot_nt(q[h], keys[at, :, cols[h]]) for keys, _, at in places]
                mine.append(dot_nt(q[h], fresh_k[:, cols[h]]))
                scores.append([jnp.where(ok, s, NEG) for ok, s in zip(allowed, mine)])
            top = [
                jnp.max(functools.reduce(jnp.maximum, mine), axis=1, keepdims=True)
                for mine in scores
            ]
            weights = [
                [jnp.exp2((s - t) * sz.factor) for s in mine] for mine, t in zip(scores, top)
            ]
            total = [jnp.sum(sum(mine), axis=1, keepdims=True) for mine in weights]
            for h in heads:
                w = [weight.astype(jnp.bfloat16) for weight in weights[h]]
                num = dot_nn(w[3], fresh_v[:, cols[h]])
                for weight, (_, values, at) in zip(w, places):
                    num = num + dot_nn(weight, values[at, :, cols[h]])
                num_ref[sz.span(request, h), :] = num
                lane = ((request - first) * sz.kv + h) * 4
                tile = jnp.where(lane_ids == lane, top[h], tile)
                tile = jnp.where(lane_ids == lane + 2, total[h], tile)
            return tile

        tile = lax.fori_loop(first, last, one, jnp.zeros((sz.rows, HD), jnp.float32))
        stat_ref[pl.ds(tile_at * sz.rows, sz.rows), :] = tile


def merge_kernel(sz, num_ref, stat_ref, came_ref, out_ref):
    for tile_at, first, last in sz.tiles():
        came_span = pl.ds(sz.all_rows + tile_at * sz.rows, sz.rows)
        mine = stat_ref[pl.ds(tile_at * sz.rows, sz.rows), :]
        came = pair_sums(came_ref[came_span, :].astype(jnp.float32))
        top = jnp.maximum(mine, came)
        keep, add = jnp.exp2((mine - top) * sz.factor), jnp.exp2((came - top) * sz.factor)
        total = mine * pltpu.roll(keep, 2, 1) + came * pltpu.roll(add, 2, 1)
        kind = lax.broadcasted_iota(jnp.int32, top.shape, 1) % 4
        put_stats(sz, out_ref, tile_at, jnp.where(kind == 0, top, total))
        for request in range(first, last):
            for head in range(sz.kv):
                lane = ((request - first) * sz.kv + head) * 4
                span = sz.span(request, head)
                joined = num_ref[span, :] * keep[:, lane : lane + 1]
                joined = joined + came_ref[span, :].astype(jnp.float32) * add[:, lane : lane + 1]
                out_ref[span, :] = joined.astype(jnp.bfloat16)


def final_kernel(sz, num_ref, stat_ref, near_ref, far_ref, out_ref, wide):
    for tile_at, first, last in sz.tiles():
        came_span = pl.ds(sz.all_rows + tile_at * sz.rows, sz.rows)
        mine = stat_ref[pl.ds(tile_at * sz.rows, sz.rows), :]
        near = pair_sums(near_ref[came_span, :].astype(jnp.float32))
        far = pair_sums(far_ref[came_span, :].astype(jnp.float32))
        top = jnp.maximum(jnp.maximum(mine, near), far)
        states = (mine, near, far)
        parts = [jnp.exp2((one - top) * sz.factor) for one in states]
        total = sum(one * pltpu.roll(part, 2, 1) for one, part in zip(states, parts))
        total = pltpu.roll(total, HD - 2, 1)
        parts = [part / total for part in parts]
        for request in range(first, last):
            for head in range(sz.kv):
                lane = ((request - first) * sz.kv + head) * 4
                span = sz.span(request, head)
                joined = sum(
                    ref[span, :].astype(jnp.float32) * part[:, lane : lane + 1]
                    for ref, part in zip((num_ref, near_ref, far_ref), parts)
                )
                for step in range(sz.steps):
                    at = (step * sz.step_rows + head * sz.group) * sz.requests
                    wide[pl.ds(at + request, sz.group, stride=sz.requests), :] = joined[
                        step * sz.group : (step + 1) * sz.group
                    ]
    for step in range(sz.steps):
        for head in range(sz.step_rows):
            at = (step * sz.step_rows + head) * sz.requests
            out_ref[step, :, head * HD : (head + 1) * HD] = wide[
                at : at + sz.requests, :
            ].astype(jnp.bfloat16)


def line_shards(
    queries,
    page_keys,
    page_values,
    page_count,
    leaf_keys,
    leaf_values,
    leaf_count,
    new_keys,
    new_values,
    path_owner,
    path_slot,
):
    requests, steps, width = queries.shape
    owners = lax.axis_size("page")
    kv = page_keys.shape[2] // HD
    pages, page_tok = page_keys.shape[:2]
    sz = Sizes(requests, steps, kv, QH // KVH, path_owner.shape[1], pages, page_tok)

    def exchange(array, hop):
        return lax.ppermute(array, "page", [(at, at ^ hop) for at in range(owners)])

    near, far = CORES, owners - CORES
    paths = jnp.concatenate([path_owner, path_slot], axis=1).astype(queries.dtype)
    paths = jnp.pad(paths, ((0, 0), (0, HD - paths.shape[1])))
    paths = jnp.broadcast_to(paths[None], (steps, requests, HD))
    block = jnp.concatenate([jnp.swapaxes(queries, 0, 1), paths], axis=2)
    far_q = exchange(block, far)
    near_q = exchange(block, near)
    mate_keys = exchange(page_keys, 1)
    mate_values = exchange(page_values, 1)
    mate_count = exchange(page_count, 1)

    smem, vmem = pltpu.SMEM, pltpu.VMEM
    sent = (jax.ShapeDtypeStruct((sz.all_rows + sz.stat_rows, HD), jnp.bfloat16),)
    exact = (
        jax.ShapeDtypeStruct((sz.all_rows, HD), jnp.float32),
        jax.ShapeDtypeStruct((sz.stat_rows, HD), jnp.float32),
    )
    wide = pltpu.VMEM((sz.all_rows, HD), jnp.float32)
    scratch = (
        wide,
        pltpu.VMEM((requests, HD), jnp.int32),
        pltpu.SMEM((requests, HD), jnp.int32),
        pltpu.SemaphoreType.DMA,
    )
    counts = (page_count, mate_count)
    all_pages = (page_keys, page_values, mate_keys, mate_values)
    flops = sz.all_rows * HD * sz.page_tok * 8
    page_bytes = 4 * page_keys.size * 2 + sz.all_rows * HD * 4

    def shared(is_exact, block):
        return plain_call(
            functools.partial(shared_kernel, sz, is_exact),
            exact if is_exact else sent,
            [smem] * 2 + [vmem] * 5,
            scratch,
            flops=flops,
            num_bytes=page_bytes,
        )(*counts, block, *all_pages)

    fresh_rows = -(-requests * steps // page_tok) * page_tok
    fresh = pltpu.VMEM((fresh_rows, kv * HD), jnp.bfloat16)
    local = plain_call(
        functools.partial(local_kernel, sz),
        exact,
        [smem] * 3 + [vmem] * 9,
        [*scratch, fresh, fresh],
        flops=flops * 2,
        num_bytes=page_bytes * 2,
    )(
        *counts,
        leaf_count,
        block,
        *all_pages,
        leaf_keys,
        leaf_values,
        jnp.swapaxes(new_keys, 0, 1),
        jnp.swapaxes(new_values, 0, 1),
    )
    far_q, local = lax.optimization_barrier((far_q, local))
    cross_q = exchange(far_q, near)
    far_part = shared(True, far_q)
    near_part = shared(False, near_q)
    cross_part = shared(False, cross_q)
    cross_back = exchange(cross_part[0], near)
    (joined,) = plain_call(
        functools.partial(merge_kernel, sz), sent, [vmem] * 3, num_bytes=sz.all_rows * HD * 8
    )(*far_part, cross_back)
    far_back = exchange(joined, far)
    near_back = exchange(near_part[0], near)
    (out,) = plain_call(
        functools.partial(final_kernel, sz),
        (jax.ShapeDtypeStruct((steps, requests, width), jnp.bfloat16),),
        [vmem] * 4,
        [wide],
        num_bytes=sz.all_rows * HD * 10,
    )(*local, near_back, far_back)
    return jnp.swapaxes(out, 0, 1)


def solution(mesh):
    on_line = mesh.shape["sub"] == 1 and mesh.shape["page"] == 4 * CORES
    return jax.shard_map(
        line_shards if on_line else shards,
        mesh=mesh,
        in_specs=(
            P(("groups", "page", "sub"), None, "head"),
            P(("groups", "page"), None, "head"),
            P(("groups", "page"), None, "head"),
            P(("groups", "page")),
            P(("groups", "page", "sub"), None, "head"),
            P(("groups", "page", "sub"), None, "head"),
            P(("groups", "page", "sub")),
            P(("groups", "page", "sub"), None, "head"),
            P(("groups", "page", "sub"), None, "head"),
            P(("groups", "page", "sub"), None),
            P(("groups", "page", "sub"), None),
        ),
        out_specs=P(("groups", "page", "sub"), None, "head"),
        check_vma=False,
    )
```

```python
import functools
import math

import jax
import jax.numpy as jnp
from jax import lax
from jax.experimental import pallas as pl
from jax.experimental.pallas import tpu as pltpu
from jax.sharding import PartitionSpec as P

HD = 128
QH = 128
KVH = 8


def page_states(query_rows, keys, values, counts):
    slot_rows = query_rows.shape[0]
    kv_local = keys.shape[2] // HD
    group_size = QH // KVH
    step_count = query_rows.shape[1] // (kv_local * group_size * HD)
    page_tok = keys.shape[1]
    query_five = query_rows.reshape(slot_rows, step_count, kv_local, group_size, HD)
    key_heads = keys.reshape(slot_rows, page_tok, kv_local, HD)
    value_heads = values.reshape(slot_rows, page_tok, kv_local, HD)
    scores = jnp.einsum(
        "nskgd,ntkd->nskgt", query_five, key_heads, preferred_element_type=jnp.float32
    ) * (1.0 / math.sqrt(HD))
    allowed = jnp.arange(page_tok, dtype=jnp.int32)[None, :] < counts[:, None]
    scores = jnp.where(allowed[:, None, None, None, :], scores, -jnp.inf)
    item_max = jnp.max(scores, axis=-1)
    weights = jnp.exp(scores - item_max[..., None])
    item_total = jnp.sum(weights, axis=-1)
    mixed = jnp.einsum(
        "nskgt,ntkd->nskgd",
        weights.astype(jnp.bfloat16),
        value_heads,
        preferred_element_type=jnp.float32,
    )
    item_out = (mixed / item_total[..., None]).astype(jnp.bfloat16)
    return (
        item_out.reshape(slot_rows, -1),
        item_max.reshape(slot_rows, -1),
        item_total.reshape(slot_rows, -1),
    )


def in_blocks(step_fn, arrays, rows_per_slot):
    owner_count = arrays[0].shape[0]
    slot_width = arrays[0].shape[1]
    wanted_slots = -(-512 // max(1, slot_width * rows_per_slot))
    divisors = [
        candidate
        for candidate in range(1, owner_count + 1)
        if owner_count % candidate == 0 and candidate >= wanted_slots
    ]
    merge_count = min(divisors)
    merged = tuple(
        (
            member.reshape(
                (owner_count // merge_count, merge_count * slot_width) + member.shape[2:]
            )
            for member in arrays
        )
    )
    results = lax.map(step_fn, merged)
    return tuple(
        (member.reshape((owner_count, slot_width) + member.shape[2:]) for member in results)
    )


def shards(
    queries,
    page_keys,
    page_values,
    page_count,
    leaf_keys,
    leaf_values,
    leaf_count,
    new_keys,
    new_values,
    path_owner,
    path_slot,
):
    request_rows, step_count, head_width = queries.shape
    kv_local = page_keys.shape[2] // HD
    group_size = QH // KVH
    page_tok = page_keys.shape[1]
    level_count = path_owner.shape[1]
    owner_count = lax.axis_size("page")
    capacity = max(
        2, min(request_rows, (2 * request_rows * level_count + owner_count - 1) // owner_count)
    )
    score_scale = 1.0 / math.sqrt(HD)
    rows_per_slot = step_count * kv_local * group_size
    item_count = request_rows * level_count
    slot_count = owner_count * capacity
    flat_owner = path_owner.reshape(item_count)
    flat_slot = path_slot.reshape(item_count)
    owner_hot = (flat_owner[:, None] == jnp.arange(owner_count, dtype=jnp.int32)[None, :]).astype(
        jnp.int32
    )
    earlier = jnp.cumsum(owner_hot, axis=0) - owner_hot
    owner_rank = jnp.sum(earlier * owner_hot, axis=1)
    position = flat_owner * capacity + owner_rank
    slot_match = (position[None, :] == jnp.arange(slot_count, dtype=jnp.int32)[:, None]).astype(
        jnp.int32
    )
    item_of_slot = jnp.sum(slot_match * jnp.arange(item_count, dtype=jnp.int32)[None, :], axis=1)
    slot_used = jnp.sum(slot_match, axis=1) > 0
    page_ids = jnp.where(slot_used, jnp.take(flat_slot, item_of_slot, axis=0), 0).reshape(
        owner_count, capacity
    )
    outgoing = jnp.take(queries, item_of_slot // level_count, axis=0).reshape(
        owner_count, capacity, step_count * head_width
    )

    def remote_block(packed):
        block_ids = packed[1]
        return page_states(
            packed[0],
            jnp.take(page_keys, block_ids, axis=0),
            jnp.take(page_values, block_ids, axis=0),
            jnp.take(page_count, block_ids, axis=0),
        )

    states = in_blocks(
        remote_block,
        (
            lax.all_to_all(outgoing, "page", split_axis=0, concat_axis=0, tiled=True),
            lax.all_to_all(page_ids, "page", split_axis=0, concat_axis=0, tiled=True),
        ),
        rows_per_slot,
    )
    out_back = lax.all_to_all(states[0], "page", split_axis=0, concat_axis=0, tiled=True)
    max_back = lax.all_to_all(states[1], "page", split_axis=0, concat_axis=0, tiled=True)
    total_back = lax.all_to_all(states[2], "page", split_axis=0, concat_axis=0, tiled=True)
    item_out = jnp.take(out_back.reshape(slot_count, step_count * head_width), position, axis=0)
    item_out = item_out.astype(jnp.float32).reshape(
        request_rows, level_count, step_count, kv_local, group_size, HD
    )
    item_max = jnp.take(max_back.reshape(slot_count, rows_per_slot), position, axis=0)
    item_max = item_max.reshape(request_rows, level_count, step_count, kv_local, group_size)
    item_total = jnp.take(total_back.reshape(slot_count, rows_per_slot), position, axis=0)
    item_total = item_total.reshape(request_rows, level_count, step_count, kv_local, group_size)
    query_five = queries.reshape(request_rows, step_count, kv_local, group_size, HD)
    leaf_heads = leaf_keys.reshape(request_rows, page_tok, kv_local, HD)
    leaf_value_heads = leaf_values.reshape(request_rows, page_tok, kv_local, HD)
    fresh_heads = new_keys.reshape(request_rows, step_count, kv_local, HD)
    fresh_value_heads = new_values.reshape(request_rows, step_count, kv_local, HD)
    leaf_scores = (
        jnp.einsum("rskgd,rtkd->rskgt", query_five, leaf_heads, preferred_element_type=jnp.float32)
        * score_scale
    )
    leaf_allowed = jnp.arange(page_tok, dtype=jnp.int32)[None, :] < leaf_count[:, None]
    leaf_scores = jnp.where(leaf_allowed[:, None, None, None, :], leaf_scores, -jnp.inf)
    fresh_scores = (
        jnp.einsum("rskgd,rukd->rskgu", query_five, fresh_heads, preferred_element_type=jnp.float32)
        * score_scale
    )
    causal = (
        jnp.arange(step_count, dtype=jnp.int32)[None, :]
        <= jnp.arange(step_count, dtype=jnp.int32)[:, None]
    )
    fresh_scores = jnp.where(causal[None, :, None, None, :], fresh_scores, -jnp.inf)
    local_max = jnp.maximum(jnp.max(leaf_scores, axis=-1), jnp.max(fresh_scores, axis=-1))
    leaf_weights = jnp.exp(leaf_scores - local_max[..., None])
    fresh_weights = jnp.exp(fresh_scores - local_max[..., None])
    local_total = jnp.sum(leaf_weights, axis=-1) + jnp.sum(fresh_weights, axis=-1)
    local_sum = jnp.einsum(
        "rskgt,rtkd->rskgd",
        leaf_weights.astype(jnp.bfloat16),
        leaf_value_heads,
        preferred_element_type=jnp.float32,
    )
    local_sum = local_sum + jnp.einsum(
        "rskgu,rukd->rskgd",
        fresh_weights.astype(jnp.bfloat16),
        fresh_value_heads,
        preferred_element_type=jnp.float32,
    )
    local_out = local_sum / local_total[..., None]
    top_score = jnp.maximum(local_max, jnp.max(item_max, axis=1))
    local_mass = local_total * jnp.exp(local_max - top_score)
    item_mass = item_total * jnp.exp(item_max - top_score[:, None])
    numerator = local_mass[..., None] * local_out + jnp.sum(item_mass[..., None] * item_out, axis=1)
    denominator = local_mass + jnp.sum(item_mass, axis=1)
    return (
        (numerator / denominator[..., None])
        .astype(jnp.bfloat16)
        .reshape(request_rows, step_count, head_width)
    )


NEG = -(2.0**127)
CORES = 2
PATH_ROWS = 16


def pair_sums(tile):
    return tile + pltpu.roll(tile, tile.shape[1] - 1, 1)


def two_pieces(values):
    high = values.astype(jnp.bfloat16).astype(jnp.float32)
    low = (values - high).astype(jnp.bfloat16).astype(jnp.float32)
    return high, low


def dot_nt(a, b):
    return lax.dot_general(a, b, (((1,), (1,)), ((), ())), preferred_element_type=jnp.float32)


def dot_nn(a, b):
    return lax.dot_general(a, b, (((1,), (0,)), ((), ())), preferred_element_type=jnp.float32)


def plain_call(kernel, out_shape, in_memory, scratch=(), flops=0, num_bytes=0):
    return pl.pallas_call(
        kernel,
        out_shape=out_shape,
        in_specs=[pl.BlockSpec(memory_space=space) for space in in_memory],
        out_specs=tuple(pl.BlockSpec(memory_space=pltpu.VMEM) for _ in out_shape),
        scratch_shapes=list(scratch),
        compiler_params=pltpu.CompilerParams(vmem_limit_bytes=16 * 1024 * 1024),
        cost_estimate=pl.CostEstimate(flops=flops, bytes_accessed=num_bytes, transcendentals=0),
    )


class Sizes:
    def __init__(self, requests, steps, kv, group, levels, pages, page_tok):
        self.requests, self.steps, self.kv, self.group = requests, steps, kv, group
        self.levels, self.pages, self.page_tok = levels, pages, page_tok
        self.rows = steps * group
        self.step_rows = kv * group
        self.all_rows = requests * kv * self.rows
        self.per_tile = HD // (4 * kv)
        self.tile_count = -(-requests // self.per_tile)
        self.stat_rows = self.tile_count * self.rows
        self.factor = 1.0 / math.sqrt(HD) * math.log2(math.e)

    def tiles(self):
        for tile_at in range(self.tile_count):
            first = tile_at * self.per_tile
            yield tile_at, first, min(self.requests, first + self.per_tile)

    def read_table(self, q_ref, counts, table_words, table_ref, sem):
        words = q_ref[self.all_rows : self.all_rows + PATH_ROWS, :]
        table_words[:PATH_ROWS, :] = words.astype(jnp.float32).astype(jnp.int32)
        for at, count_ref in enumerate(counts):
            table_words[PATH_ROWS + at : PATH_ROWS + at + 1, : self.pages] = count_ref[...].reshape(1, self.pages)
        copy = pltpu.make_async_copy(table_words, table_ref, sem)
        copy.start()
        return copy

    def span(self, request, kv_head):
        at = (request * self.kv + kv_head) * self.rows
        return pl.ds(at if isinstance(at, int) else pl.multiple_of(at, 16), self.rows)

    def find(self, table_ref, owner, which, request):
        slot, used = jnp.int32(0), jnp.int32(0)
        for level in range(self.levels):
            hit = table_ref[level, request] == owner
            slot = jnp.where(hit, table_ref[self.levels + level, request], slot)
            used = jnp.where(hit, 1, used)
        return slot, used * table_ref[PATH_ROWS + which, slot]


def shared_kernel(
    sz, chunk, exact, count0_ref, count1_ref, q_ref, k0, v0, k1, v1, *rest
):
    *outs, table_words, table_ref, sem = rest
    num_ref = outs[0]
    me = lax.axis_index("page")
    mate = jnp.bitwise_xor(me, 1)
    lane_ids = lax.broadcasted_iota(jnp.int32, (sz.rows, HD), 1)
    token_ids = lax.broadcasted_iota(jnp.int32, (sz.rows, sz.page_tok), 1)
    heads = range(sz.kv)
    copy = sz.read_table(q_ref, (count0_ref, count1_ref), table_words, table_ref, sem)
    copy.wait()
    for tile_at, first, last in sz.tiles():
        tile = jnp.zeros((sz.rows, HD), jnp.float32)
        for start in range(first, last, 4):
            items = []
            for request in range(start, min(last, start + 4)):
                slot0, count0 = sz.find(table_ref, me, 0, chunk * sz.requests + request)
                slot1, count1 = sz.find(table_ref, mate, 1, chunk * sz.requests + request)
                allowed = jnp.concatenate([token_ids < count0, token_ids < count1], axis=1)
                items += [(request, head, slot0, slot1, allowed) for head in heads]
            scores = []
            for request, head, slot0, slot1, allowed in items:
                cols = slice(head * HD, (head + 1) * HD)
                keys = jnp.concatenate([k0[slot0, :, cols], k1[slot1, :, cols]], 0)
                s = dot_nt(q_ref[sz.span(request, head), :], keys)
                scores.append(jnp.where(allowed, s, NEG))
            point = [sum(two_pieces(jnp.max(s, axis=1, keepdims=True))) for s in scores]
            weights = [jnp.exp2((s - p) * sz.factor) for s, p in zip(scores, point)]
            total = [jnp.sum(w, axis=1, keepdims=True) for w in weights]
            for at, (request, head, slot0, slot1, _) in enumerate(items):
                cols = slice(head * HD, (head + 1) * HD)
                values = jnp.concatenate([v0[slot0, :, cols], v1[slot1, :, cols]], 0)
                num = dot_nn(weights[at].astype(jnp.bfloat16), values)
                num_ref[sz.span(request, head), :] = num.astype(num_ref.dtype)
                lane = ((request - first) * sz.kv + head) * 4
                tile = jnp.where(lane_ids == lane, point[at], tile)
                tile = jnp.where(lane_ids == lane + 2, total[at], tile)
        if exact:
            outs[1][pl.ds(tile_at * sz.rows, sz.rows), :] = tile
        else:
            put_stats(sz, num_ref, tile_at, tile)


def put_stats(sz, out_ref, tile_at, tile):
    kind = lax.broadcasted_iota(jnp.int32, tile.shape, 1) % 4
    high, low = two_pieces(tile)
    tile = jnp.where(kind % 2 == 0, high, pltpu.roll(low, 1, 1))
    out_ref[pl.ds(sz.all_rows + tile_at * sz.rows, sz.rows), :] = tile.astype(jnp.bfloat16)


def local_kernel(
    sz,
    chunk,
    count0_ref,
    count1_ref,
    leaf_count_ref,
    q_ref,
    k0,
    v0,
    k1,
    v1,
    leaf_k_any,
    leaf_v_any,
    new_k,
    new_v,
    num_ref,
    stat_ref,
    table_words,
    table_ref,
    sem,
    fresh_k,
    fresh_v,
    leaf_k,
    leaf_v,
    leaf_sem,
):
    def leaf_copy(request, whole, part, sem_at):
        return pltpu.make_async_copy(
            whole.at[chunk * sz.requests + request], part.at[request], leaf_sem.at[request, sem_at]
        )

    for request in range(sz.requests):
        leaf_copy(request, leaf_k_any, leaf_k, 0).start()
        leaf_copy(request, leaf_v_any, leaf_v, 1).start()
    me = lax.axis_index("page")
    mate = jnp.bitwise_xor(me, 1)
    lane_ids = lax.broadcasted_iota(jnp.int32, (sz.rows, HD), 1)
    token_ids = lax.broadcasted_iota(jnp.int32, (sz.rows, sz.page_tok), 1)
    fresh = fresh_k.shape[0]
    fresh_ids = lax.broadcasted_iota(jnp.int32, (sz.rows, fresh), 1)
    step_ids = lax.broadcasted_iota(jnp.int32, (sz.rows, fresh), 0) // sz.group
    device_requests = new_k.shape[1]
    causal = (fresh_ids // device_requests) <= step_ids
    fresh_request = fresh_ids % device_requests
    heads = range(sz.kv)
    cols = [slice(head * HD, (head + 1) * HD) for head in heads]
    copy = sz.read_table(q_ref, (count0_ref, count1_ref), table_words, table_ref, sem)
    copy.wait()
    for new_ref, full in ((new_k, fresh_k), (new_v, fresh_v)):
        rows = [new_ref[step].astype(jnp.float32) for step in range(sz.steps)]
        filler = fresh - sz.steps * device_requests
        if filler:
            rows.append(jnp.zeros((filler, sz.kv * HD), jnp.float32))
        full[...] = jnp.concatenate(rows, axis=0).astype(full.dtype)
    for tile_at, first, last in sz.tiles():
        tile = jnp.zeros((sz.rows, HD), jnp.float32)
        for start in range(first, last, 2):
            items = []
            for request in range(start, min(last, start + 2)):
                row = chunk * sz.requests + request
                slot0, count0 = sz.find(table_ref, me, 0, row)
                slot1, count1 = sz.find(table_ref, mate, 1, row)
                allowed = (
                    token_ids < count0,
                    token_ids < count1,
                    token_ids < leaf_count_ref[row],
                    causal & (fresh_request == row),
                )
                allowed = jnp.concatenate(allowed, axis=1)
                places = ((k0, v0, slot0), (k1, v1, slot1), (leaf_k, leaf_v, request))
                items += [(request, head, places, allowed) for head in heads]
                leaf_copy(request, leaf_k_any, leaf_k, 0).wait()
                leaf_copy(request, leaf_v_any, leaf_v, 1).wait()
            scores = []
            for request, head, places, allowed in items:
                keys = [keys[at, :, cols[head]] for keys, _, at in places]
                keys = jnp.concatenate(keys + [fresh_k[:, cols[head]]], 0)
                s = dot_nt(q_ref[sz.span(request, head), :], keys)
                scores.append(jnp.where(allowed, s, NEG))
            top = [jnp.max(s, axis=1, keepdims=True) for s in scores]
            weights = [jnp.exp2((s - t) * sz.factor) for s, t in zip(scores, top)]
            total = [jnp.sum(w, axis=1, keepdims=True) for w in weights]
            for at, (request, head, places, _) in enumerate(items):
                values = [values[slot, :, cols[head]] for _, values, slot in places]
                values = jnp.concatenate(values + [fresh_v[:, cols[head]]], 0)
                num_ref[sz.span(request, head), :] = dot_nn(
                    weights[at].astype(jnp.bfloat16), values
                )
                lane = ((request - first) * sz.kv + head) * 4
                tile = jnp.where(lane_ids == lane, top[at], tile)
                tile = jnp.where(lane_ids == lane + 2, total[at], tile)
        stat_ref[pl.ds(tile_at * sz.rows, sz.rows), :] = tile


def merge_kernel(sz, num_ref, stat_ref, came_ref, out_ref):
    for tile_at, first, last in sz.tiles():
        came_span = pl.ds(sz.all_rows + tile_at * sz.rows, sz.rows)
        mine = stat_ref[pl.ds(tile_at * sz.rows, sz.rows), :]
        came = pair_sums(came_ref[came_span, :].astype(jnp.float32))
        top = jnp.maximum(mine, came)
        keep, add = jnp.exp2((mine - top) * sz.factor), jnp.exp2((came - top) * sz.factor)
        total = mine * pltpu.roll(keep, 2, 1) + came * pltpu.roll(add, 2, 1)
        kind = lax.broadcasted_iota(jnp.int32, top.shape, 1) % 4
        put_stats(sz, out_ref, tile_at, jnp.where(kind == 0, top, total))
        for request in range(first, last):
            for head in range(sz.kv):
                lane = ((request - first) * sz.kv + head) * 4
                span = sz.span(request, head)
                joined = num_ref[span, :] * keep[:, lane : lane + 1]
                joined = joined + came_ref[span, :].astype(jnp.float32) * add[:, lane : lane + 1]
                out_ref[span, :] = joined.astype(jnp.bfloat16)


def join_kernel(sz, num_ref, stat_ref, came_ref, out_ref, out_stat_ref):
    mine = stat_ref[...]
    came = pair_sums(came_ref[sz.all_rows : sz.all_rows + sz.rows, :].astype(jnp.float32))
    top = jnp.maximum(mine, came)
    keep, add = jnp.exp2((mine - top) * sz.factor), jnp.exp2((came - top) * sz.factor)
    total = mine * pltpu.roll(keep, 2, 1) + came * pltpu.roll(add, 2, 1)
    kind = lax.broadcasted_iota(jnp.int32, top.shape, 1) % 4
    out_stat_ref[...] = jnp.where(kind == 0, top, total)
    for request in range(sz.requests):
        for head in range(sz.kv):
            lane = (request * sz.kv + head) * 4
            span = sz.span(request, head)
            joined = num_ref[span, :] * keep[:, lane : lane + 1]
            out_ref[span, :] = joined + came_ref[span, :].astype(jnp.float32) * add[
                :, lane : lane + 1
            ]


def final_kernel(whole, sz, num_ref, stat_ref, *refs):
    *came_refs, out_ref, wide = refs
    lanes = sz.requests * sz.kv * 4
    lane_ids = lax.broadcasted_iota(jnp.int32, (sz.rows, HD), 1)
    mine = stat_ref[...]
    came = jnp.zeros((sz.rows, HD), jnp.float32)
    for chunk, came_ref in enumerate(came_refs):
        tile = pair_sums(came_ref[sz.all_rows : sz.all_rows + sz.rows, :].astype(jnp.float32))
        if chunk:
            tile = pltpu.roll(tile, chunk * lanes, 1)
        came = jnp.where(lane_ids // lanes == chunk, tile, came)
    top = jnp.maximum(mine, came)
    keep, add = jnp.exp2((mine - top) * sz.factor), jnp.exp2((came - top) * sz.factor)
    total = mine * pltpu.roll(keep, 2, 1) + came * pltpu.roll(add, 2, 1)
    total = pltpu.roll(total, HD - 2, 1)
    keep, add = keep / total, add / total
    for row in range(whole.requests):
        chunk, request = row // sz.requests, row % sz.requests
        for head in range(sz.kv):
            lane = (row * sz.kv + head) * 4
            joined = num_ref[whole.span(row, head), :] * keep[:, lane : lane + 1]
            joined = joined + came_refs[chunk][sz.span(request, head), :].astype(
                jnp.float32
            ) * add[:, lane : lane + 1]
            for step in range(sz.steps):
                at = (step * sz.step_rows + head * sz.group) * whole.requests
                wide[pl.ds(at + row, sz.group, stride=whole.requests), :] = joined[
                    step * sz.group : (step + 1) * sz.group
                ]
    for step in range(sz.steps):
        for head in range(sz.step_rows):
            at = (step * sz.step_rows + head) * whole.requests
            out_ref[step, :, head * HD : (head + 1) * HD] = wide[
                at : at + whole.requests, :
            ].astype(jnp.bfloat16)


def fetch_kernel(k_any, v_any, k_ref, v_ref, sems):
    copies = [
        pltpu.make_async_copy(source, target, sems.at[at])
        for at, (source, target) in enumerate(((k_any, k_ref), (v_any, v_ref)))
    ]
    for copy in copies:
        copy.start()
    for copy in copies:
        copy.wait()


def pack_kernel(sz, chunks, q_ref, owner_ref, slot_ref, *refs):
    *outs, wide, words = refs
    all_requests = chunks * sz.requests
    words[...] = jnp.zeros(words.shape, words.dtype)
    words[: sz.levels, :all_requests] = owner_ref[...]
    words[sz.levels : 2 * sz.levels, :all_requests] = slot_ref[...]
    paths = words[...].astype(jnp.float32).astype(jnp.bfloat16)
    for out in outs:
        out[sz.all_rows : sz.all_rows + PATH_ROWS, :] = paths
    for step in range(sz.steps):
        for head in range(sz.step_rows):
            at = (step * sz.step_rows + head) * all_requests
            wide[at : at + all_requests, :] = q_ref[
                step, :, head * HD : (head + 1) * HD
            ].astype(jnp.float32)
    for chunk, out in enumerate(outs):
        for request in range(sz.requests):
            for head in range(sz.kv):
                parts = []
                for step in range(sz.steps):
                    at = (step * sz.step_rows + head * sz.group) * all_requests
                    at = at + chunk * sz.requests + request
                    parts.append(wide[pl.ds(at, sz.group, stride=all_requests), :])
                rows = jnp.concatenate(parts, axis=0).astype(out.dtype)
                out[sz.span(request, head), :] = rows


def line_shards(
    queries,
    page_keys,
    page_values,
    page_count,
    leaf_keys,
    leaf_values,
    leaf_count,
    new_keys,
    new_values,
    path_owner,
    path_slot,
):
    requests, steps, width = queries.shape
    owners = lax.axis_size("page")
    kv = page_keys.shape[2] // HD
    pages, page_tok = page_keys.shape[:2]
    chunks = 1
    line = (queries, page_keys, page_values, page_count, leaf_keys, leaf_values, leaf_count)
    if requests % chunks or requests * kv * 4 != HD:
        return shards(*line, new_keys, new_values, path_owner, path_slot)
    shape_of = (steps, kv, QH // KVH, path_owner.shape[1], pages, page_tok)
    whole, sz = Sizes(requests, *shape_of), Sizes(requests // chunks, *shape_of)

    def exchange(array, hop):
        return lax.ppermute(array, "page", [(at, at ^ hop) for at in range(owners)])

    def after(array, *others):
        return lax.optimization_barrier((array, *others))[0]

    near, far = CORES, owners - CORES
    smem, vmem, hbm = pltpu.SMEM, pltpu.VMEM, pl.ANY
    shape = jax.ShapeDtypeStruct
    scratch = (
        pltpu.VMEM((PATH_ROWS + 8, HD), jnp.int32),
        pltpu.SMEM((PATH_ROWS + 8, HD), jnp.int32),
        pltpu.SemaphoreType.DMA,
    )
    wide = pltpu.VMEM((whole.all_rows, HD), jnp.float32)
    fresh_rows = -(-requests * steps // page_tok) * page_tok
    fresh = pltpu.VMEM((fresh_rows, kv * HD), jnp.bfloat16)
    leaves = pltpu.VMEM((requests, page_tok, kv * HD), jnp.bfloat16)

    def sent(size):
        return (shape((size.all_rows + size.stat_rows, HD), jnp.bfloat16),)

    def exact(size):
        return (
            shape((size.all_rows, HD), jnp.float32),
            shape((size.stat_rows, HD), jnp.float32),
        )

    (block,) = plain_call(
        functools.partial(pack_kernel, sz, chunks),
        (shape((whole.all_rows + PATH_ROWS, HD), jnp.bfloat16),),
        [vmem] * 3,
        [wide, pltpu.VMEM((PATH_ROWS, HD), jnp.int32)],
    )(*(jnp.swapaxes(array, 0, 1) for array in (queries, path_owner, path_slot)))
    far_q = exchange(block, far)
    near_q = exchange(block, near)
    mate_keys, mate_values, mate_count = (
        exchange(array, 1) for array in (page_keys, page_values, page_count)
    )
    counts = (page_count, mate_count)
    own_pages = plain_call(
        fetch_kernel,
        (shape(page_keys.shape, page_keys.dtype),) * 2,
        [hbm] * 2,
        [pltpu.SemaphoreType.DMA((2,))],
    )(after(page_keys, block), page_values)
    all_pages = (*own_pages, mate_keys, mate_values)
    far_q = after(far_q, *all_pages, mate_count)

    def shared(size, chunk, is_exact, rows):
        return plain_call(
            functools.partial(shared_kernel, size, chunk, is_exact),
            exact(size) if is_exact else sent(size),
            [vmem] * 7,
            scratch,
        )(*counts, rows, *all_pages)

    def merge(part, came):
        return plain_call(functools.partial(merge_kernel, sz), sent(sz), [vmem] * 3)(*part, came)[0]

    cross_q = exchange(far_q, near)
    near_q = after(near_q, far_q)
    far_part = shared(sz, 0, True, after(far_q, near_q))
    cross_q = after(cross_q, *far_part)
    cross_part = shared(sz, 0, False, cross_q)[0]
    cross_back = exchange(cross_part, near)
    near_part = shared(sz, 0, False, after(near_q, cross_part))[0]
    cross_back = after(cross_back, near_part)
    joined = merge(far_part, cross_back)
    far_back = exchange(joined, far)
    near_back = exchange(after(near_part, joined), near)
    local = plain_call(
        functools.partial(local_kernel, whole, 0),
        exact(whole),
        [vmem] * 2 + [smem] + [vmem] * 5 + [hbm] * 2 + [vmem] * 2,
        [*scratch, fresh, fresh, leaves, leaves, pltpu.SemaphoreType.DMA((requests, 2))],
    )(
        *counts,
        leaf_count,
        after(block, joined),
        *all_pages,
        leaf_keys,
        leaf_values,
        jnp.swapaxes(new_keys, 0, 1),
        jnp.swapaxes(new_values, 0, 1),
    )
    state = plain_call(functools.partial(join_kernel, whole), exact(whole), [vmem] * 3)(
        *local, after(near_back, *local)
    )
    (out,) = plain_call(
        functools.partial(final_kernel, whole, sz),
        (shape((steps, requests, width), jnp.bfloat16),),
        [vmem] * 3,
        [wide],
    )(*state, far_back)
    return jnp.swapaxes(out, 0, 1)


def solution(mesh):
    on_line = mesh.shape["sub"] == 1 and mesh.shape["page"] == 4 * CORES
    return jax.shard_map(
        line_shards if on_line else shards,
        mesh=mesh,
        in_specs=(
            P(("groups", "page", "sub"), None, "head"),
            P(("groups", "page"), None, "head"),
            P(("groups", "page"), None, "head"),
            P(("groups", "page")),
            P(("groups", "page", "sub"), None, "head"),
            P(("groups", "page", "sub"), None, "head"),
            P(("groups", "page", "sub")),
            P(("groups", "page", "sub"), None, "head"),
            P(("groups", "page", "sub"), None, "head"),
            P(("groups", "page", "sub"), None),
            P(("groups", "page", "sub"), None),
        ),
        out_specs=P(("groups", "page", "sub"), None, "head"),
        check_vma=False,
    )
```

```python
import functools
import math

import jax
import jax.numpy as jnp
from jax import lax
from jax.experimental import pallas as pl
from jax.experimental.pallas import tpu as pltpu
from jax.sharding import PartitionSpec as P

HD = 128
QH = 128
KVH = 8


def page_states(query_rows, keys, values, counts):
    slot_rows = query_rows.shape[0]
    kv_local = keys.shape[2] // HD
    group_size = QH // KVH
    step_count = query_rows.shape[1] // (kv_local * group_size * HD)
    page_tok = keys.shape[1]
    query_five = query_rows.reshape(slot_rows, step_count, kv_local, group_size, HD)
    key_heads = keys.reshape(slot_rows, page_tok, kv_local, HD)
    value_heads = values.reshape(slot_rows, page_tok, kv_local, HD)
    scores = jnp.einsum(
        "nskgd,ntkd->nskgt", query_five, key_heads, preferred_element_type=jnp.float32
    ) * (1.0 / math.sqrt(HD))
    allowed = jnp.arange(page_tok, dtype=jnp.int32)[None, :] < counts[:, None]
    scores = jnp.where(allowed[:, None, None, None, :], scores, -jnp.inf)
    item_max = jnp.max(scores, axis=-1)
    weights = jnp.exp(scores - item_max[..., None])
    item_total = jnp.sum(weights, axis=-1)
    mixed = jnp.einsum(
        "nskgt,ntkd->nskgd",
        weights.astype(jnp.bfloat16),
        value_heads,
        preferred_element_type=jnp.float32,
    )
    item_out = (mixed / item_total[..., None]).astype(jnp.bfloat16)
    return (
        item_out.reshape(slot_rows, -1),
        item_max.reshape(slot_rows, -1),
        item_total.reshape(slot_rows, -1),
    )


def in_blocks(step_fn, arrays, rows_per_slot):
    owner_count = arrays[0].shape[0]
    slot_width = arrays[0].shape[1]
    wanted_slots = -(-512 // max(1, slot_width * rows_per_slot))
    divisors = [
        candidate
        for candidate in range(1, owner_count + 1)
        if owner_count % candidate == 0 and candidate >= wanted_slots
    ]
    merge_count = min(divisors)
    merged = tuple(
        (
            member.reshape(
                (owner_count // merge_count, merge_count * slot_width) + member.shape[2:]
            )
            for member in arrays
        )
    )
    results = lax.map(step_fn, merged)
    return tuple(
        (member.reshape((owner_count, slot_width) + member.shape[2:]) for member in results)
    )


def shards(
    queries,
    page_keys,
    page_values,
    page_count,
    leaf_keys,
    leaf_values,
    leaf_count,
    new_keys,
    new_values,
    path_owner,
    path_slot,
):
    request_rows, step_count, head_width = queries.shape
    kv_local = page_keys.shape[2] // HD
    group_size = QH // KVH
    page_tok = page_keys.shape[1]
    level_count = path_owner.shape[1]
    owner_count = lax.axis_size("page")
    capacity = max(
        2, min(request_rows, (2 * request_rows * level_count + owner_count - 1) // owner_count)
    )
    score_scale = 1.0 / math.sqrt(HD)
    rows_per_slot = step_count * kv_local * group_size
    item_count = request_rows * level_count
    slot_count = owner_count * capacity
    flat_owner = path_owner.reshape(item_count)
    flat_slot = path_slot.reshape(item_count)
    owner_hot = (flat_owner[:, None] == jnp.arange(owner_count, dtype=jnp.int32)[None, :]).astype(
        jnp.int32
    )
    earlier = jnp.cumsum(owner_hot, axis=0) - owner_hot
    owner_rank = jnp.sum(earlier * owner_hot, axis=1)
    position = flat_owner * capacity + owner_rank
    slot_match = (position[None, :] == jnp.arange(slot_count, dtype=jnp.int32)[:, None]).astype(
        jnp.int32
    )
    item_of_slot = jnp.sum(slot_match * jnp.arange(item_count, dtype=jnp.int32)[None, :], axis=1)
    slot_used = jnp.sum(slot_match, axis=1) > 0
    page_ids = jnp.where(slot_used, jnp.take(flat_slot, item_of_slot, axis=0), 0).reshape(
        owner_count, capacity
    )
    outgoing = jnp.take(queries, item_of_slot // level_count, axis=0).reshape(
        owner_count, capacity, step_count * head_width
    )

    def remote_block(packed):
        block_ids = packed[1]
        return page_states(
            packed[0],
            jnp.take(page_keys, block_ids, axis=0),
            jnp.take(page_values, block_ids, axis=0),
            jnp.take(page_count, block_ids, axis=0),
        )

    states = in_blocks(
        remote_block,
        (
            lax.all_to_all(outgoing, "page", split_axis=0, concat_axis=0, tiled=True),
            lax.all_to_all(page_ids, "page", split_axis=0, concat_axis=0, tiled=True),
        ),
        rows_per_slot,
    )
    out_back = lax.all_to_all(states[0], "page", split_axis=0, concat_axis=0, tiled=True)
    max_back = lax.all_to_all(states[1], "page", split_axis=0, concat_axis=0, tiled=True)
    total_back = lax.all_to_all(states[2], "page", split_axis=0, concat_axis=0, tiled=True)
    item_out = jnp.take(out_back.reshape(slot_count, step_count * head_width), position, axis=0)
    item_out = item_out.astype(jnp.float32).reshape(
        request_rows, level_count, step_count, kv_local, group_size, HD
    )
    item_max = jnp.take(max_back.reshape(slot_count, rows_per_slot), position, axis=0)
    item_max = item_max.reshape(request_rows, level_count, step_count, kv_local, group_size)
    item_total = jnp.take(total_back.reshape(slot_count, rows_per_slot), position, axis=0)
    item_total = item_total.reshape(request_rows, level_count, step_count, kv_local, group_size)
    query_five = queries.reshape(request_rows, step_count, kv_local, group_size, HD)
    leaf_heads = leaf_keys.reshape(request_rows, page_tok, kv_local, HD)
    leaf_value_heads = leaf_values.reshape(request_rows, page_tok, kv_local, HD)
    fresh_heads = new_keys.reshape(request_rows, step_count, kv_local, HD)
    fresh_value_heads = new_values.reshape(request_rows, step_count, kv_local, HD)
    leaf_scores = (
        jnp.einsum("rskgd,rtkd->rskgt", query_five, leaf_heads, preferred_element_type=jnp.float32)
        * score_scale
    )
    leaf_allowed = jnp.arange(page_tok, dtype=jnp.int32)[None, :] < leaf_count[:, None]
    leaf_scores = jnp.where(leaf_allowed[:, None, None, None, :], leaf_scores, -jnp.inf)
    fresh_scores = (
        jnp.einsum("rskgd,rukd->rskgu", query_five, fresh_heads, preferred_element_type=jnp.float32)
        * score_scale
    )
    causal = (
        jnp.arange(step_count, dtype=jnp.int32)[None, :]
        <= jnp.arange(step_count, dtype=jnp.int32)[:, None]
    )
    fresh_scores = jnp.where(causal[None, :, None, None, :], fresh_scores, -jnp.inf)
    local_max = jnp.maximum(jnp.max(leaf_scores, axis=-1), jnp.max(fresh_scores, axis=-1))
    leaf_weights = jnp.exp(leaf_scores - local_max[..., None])
    fresh_weights = jnp.exp(fresh_scores - local_max[..., None])
    local_total = jnp.sum(leaf_weights, axis=-1) + jnp.sum(fresh_weights, axis=-1)
    local_sum = jnp.einsum(
        "rskgt,rtkd->rskgd",
        leaf_weights.astype(jnp.bfloat16),
        leaf_value_heads,
        preferred_element_type=jnp.float32,
    )
    local_sum = local_sum + jnp.einsum(
        "rskgu,rukd->rskgd",
        fresh_weights.astype(jnp.bfloat16),
        fresh_value_heads,
        preferred_element_type=jnp.float32,
    )
    local_out = local_sum / local_total[..., None]
    top_score = jnp.maximum(local_max, jnp.max(item_max, axis=1))
    local_mass = local_total * jnp.exp(local_max - top_score)
    item_mass = item_total * jnp.exp(item_max - top_score[:, None])
    numerator = local_mass[..., None] * local_out + jnp.sum(item_mass[..., None] * item_out, axis=1)
    denominator = local_mass + jnp.sum(item_mass, axis=1)
    return (
        (numerator / denominator[..., None])
        .astype(jnp.bfloat16)
        .reshape(request_rows, step_count, head_width)
    )


NEG = -(2.0**127)
CORES = 2


def pair_sums(tile):
    return tile + pltpu.roll(tile, tile.shape[1] - 1, 1)


def two_pieces(values):
    high = values.astype(jnp.bfloat16).astype(jnp.float32)
    low = (values - high).astype(jnp.bfloat16).astype(jnp.float32)
    return high, low


def dot_nt(a, b):
    return lax.dot_general(a, b, (((1,), (1,)), ((), ())), preferred_element_type=jnp.float32)


def dot_nn(a, b):
    return lax.dot_general(a, b, (((1,), (0,)), ((), ())), preferred_element_type=jnp.float32)


def plain_call(kernel, out_shape, in_memory, scratch=(), flops=0, num_bytes=0):
    return pl.pallas_call(
        kernel,
        out_shape=out_shape,
        in_specs=[pl.BlockSpec(memory_space=space) for space in in_memory],
        out_specs=tuple(pl.BlockSpec(memory_space=pltpu.VMEM) for _ in out_shape),
        scratch_shapes=list(scratch),
        compiler_params=pltpu.CompilerParams(vmem_limit_bytes=16 * 1024 * 1024),
        cost_estimate=pl.CostEstimate(flops=flops, bytes_accessed=num_bytes, transcendentals=0),
    )


class Sizes:
    def __init__(self, requests, steps, kv, group, levels, pages, page_tok):
        self.requests, self.steps, self.kv, self.group = requests, steps, kv, group
        self.levels, self.pages, self.page_tok = levels, pages, page_tok
        self.rows = steps * group
        self.step_rows = kv * group
        self.all_rows = requests * kv * self.rows
        self.per_tile = HD // (4 * kv)
        self.tile_count = -(-requests // self.per_tile)
        self.stat_rows = self.tile_count * self.rows
        self.factor = 1.0 / math.sqrt(HD) * math.log2(math.e)

    def tiles(self):
        for tile_at in range(self.tile_count):
            first = tile_at * self.per_tile
            yield tile_at, first, min(self.requests, first + self.per_tile)

    def spread(self, q_ref, wide):
        for step in range(self.steps):
            for head in range(self.step_rows):
                at = (step * self.step_rows + head) * self.requests
                wide[at : at + self.requests, :] = q_ref[
                    step, :, head * HD : (head + 1) * HD
                ].astype(jnp.float32)

    def pick(self, wide, request, kv_head):
        parts = []
        for step in range(self.steps):
            at = (step * self.step_rows + kv_head * self.group) * self.requests
            parts.append(wide[pl.ds(at + request, self.group, stride=self.requests), :])
        return jnp.concatenate(parts, axis=0).astype(jnp.bfloat16)

    def span(self, request, kv_head):
        at = (request * self.kv + kv_head) * self.rows
        return pl.ds(at if isinstance(at, int) else pl.multiple_of(at, 16), self.rows)

    def find(self, table_ref, count_ref, owner, request):
        slot, used = jnp.int32(0), jnp.int32(0)
        for level in range(self.levels):
            index = table_ref[level, request]
            hit = index // self.pages == owner
            slot = jnp.where(hit, index % self.pages, slot)
            used = jnp.where(hit, 1, used)
        return slot, used * count_ref[slot]


def shared_kernel(
    sz, chunk, exact, table_ref, count0_ref, count1_ref, q_ref, k0, v0, k1, v1, *rest
):
    *outs, wide = rest
    num_ref = outs[0]
    me = lax.axis_index("page")
    mate = jnp.bitwise_xor(me, 1)
    lane_ids = lax.broadcasted_iota(jnp.int32, (sz.rows, HD), 1)
    token_ids = lax.broadcasted_iota(jnp.int32, (sz.rows, sz.page_tok), 1)
    heads = range(sz.kv)
    sz.spread(q_ref, wide)
    for tile_at, first, last in sz.tiles():
        tile = jnp.zeros((sz.rows, HD), jnp.float32)
        for start in range(first, last, 4):
            items = []
            for request in range(start, min(last, start + 4)):
                slot0, count0 = sz.find(table_ref, count0_ref, me, request)
                slot1, count1 = sz.find(table_ref, count1_ref, mate, request)
                allowed = jnp.concatenate([token_ids < count0, token_ids < count1], axis=1)
                items += [(request, head, slot0, slot1, allowed) for head in heads]
            scores = []
            for request, head, slot0, slot1, allowed in items:
                cols = slice(head * HD, (head + 1) * HD)
                keys = jnp.concatenate([k0[slot0, :, cols], k1[slot1, :, cols]], 0)
                s = dot_nt(sz.pick(wide, request, head), keys)
                scores.append(jnp.where(allowed, s, NEG))
            point = [sum(two_pieces(jnp.max(s, axis=1, keepdims=True))) for s in scores]
            weights = [jnp.exp2((s - p) * sz.factor) for s, p in zip(scores, point)]
            total = [jnp.sum(w, axis=1, keepdims=True) for w in weights]
            for at, (request, head, slot0, slot1, _) in enumerate(items):
                cols = slice(head * HD, (head + 1) * HD)
                values = jnp.concatenate([v0[slot0, :, cols], v1[slot1, :, cols]], 0)
                num = dot_nn(weights[at].astype(jnp.bfloat16), values)
                num_ref[sz.span(request, head), :] = num.astype(num_ref.dtype)
                lane = ((request - first) * sz.kv + head) * 4
                tile = jnp.where(lane_ids == lane, point[at], tile)
                tile = jnp.where(lane_ids == lane + 2, total[at], tile)
        if exact:
            outs[1][pl.ds(tile_at * sz.rows, sz.rows), :] = tile
        else:
            put_stats(sz, num_ref, tile_at, tile)


def put_stats(sz, out_ref, tile_at, tile):
    kind = lax.broadcasted_iota(jnp.int32, tile.shape, 1) % 4
    high, low = two_pieces(tile)
    tile = jnp.where(kind % 2 == 0, high, pltpu.roll(low, 1, 1))
    out_ref[pl.ds(sz.all_rows + tile_at * sz.rows, sz.rows), :] = tile.astype(jnp.bfloat16)


def local_kernel(
    sz,
    chunk,
    table_ref,
    count0_ref,
    count1_ref,
    leaf_count_ref,
    q_ref,
    k0,
    v0,
    k1,
    v1,
    leaf_k_any,
    leaf_v_any,
    new_k,
    new_v,
    num_ref,
    stat_ref,
    wide,
    fresh_k,
    fresh_v,
    leaf_k,
    leaf_v,
    leaf_sem,
):
    def leaf_copy(request, whole, part, sem_at):
        return pltpu.make_async_copy(
            whole.at[chunk * sz.requests + request], part.at[request], leaf_sem.at[request, sem_at]
        )

    for request in range(sz.requests):
        leaf_copy(request, leaf_k_any, leaf_k, 0).start()
        leaf_copy(request, leaf_v_any, leaf_v, 1).start()
    me = lax.axis_index("page")
    mate = jnp.bitwise_xor(me, 1)
    lane_ids = lax.broadcasted_iota(jnp.int32, (sz.rows, HD), 1)
    token_ids = lax.broadcasted_iota(jnp.int32, (sz.rows, sz.page_tok), 1)
    fresh = fresh_k.shape[0]
    fresh_ids = lax.broadcasted_iota(jnp.int32, (sz.rows, fresh), 1)
    step_ids = lax.broadcasted_iota(jnp.int32, (sz.rows, fresh), 0) // sz.group
    device_requests = new_k.shape[1]
    causal = (fresh_ids // device_requests) <= step_ids
    fresh_request = fresh_ids % device_requests
    heads = range(sz.kv)
    cols = [slice(head * HD, (head + 1) * HD) for head in heads]
    sz.spread(q_ref, wide)
    for new_ref, full in ((new_k, fresh_k), (new_v, fresh_v)):
        rows = [new_ref[step].astype(jnp.float32) for step in range(sz.steps)]
        filler = fresh - sz.steps * device_requests
        if filler:
            rows.append(jnp.zeros((filler, sz.kv * HD), jnp.float32))
        full[...] = jnp.concatenate(rows, axis=0).astype(full.dtype)
    for tile_at, first, last in sz.tiles():
        tile = jnp.zeros((sz.rows, HD), jnp.float32)
        for start in range(first, last, 2):
            items = []
            for request in range(start, min(last, start + 2)):
                row = chunk * sz.requests + request
                slot0, count0 = sz.find(table_ref, count0_ref, me, row)
                slot1, count1 = sz.find(table_ref, count1_ref, mate, row)
                allowed = (
                    token_ids < count0,
                    token_ids < count1,
                    token_ids < leaf_count_ref[row],
                    causal & (fresh_request == row),
                )
                allowed = jnp.concatenate(allowed, axis=1)
                places = ((k0, v0, slot0), (k1, v1, slot1), (leaf_k, leaf_v, request))
                items += [(request, head, places, allowed) for head in heads]
                leaf_copy(request, leaf_k_any, leaf_k, 0).wait()
                leaf_copy(request, leaf_v_any, leaf_v, 1).wait()
            scores = []
            for request, head, places, allowed in items:
                keys = [keys[at, :, cols[head]] for keys, _, at in places]
                keys = jnp.concatenate(keys + [fresh_k[:, cols[head]]], 0)
                s = dot_nt(sz.pick(wide, request, head), keys)
                scores.append(jnp.where(allowed, s, NEG))
            top = [jnp.max(s, axis=1, keepdims=True) for s in scores]
            weights = [jnp.exp2((s - t) * sz.factor) for s, t in zip(scores, top)]
            total = [jnp.sum(w, axis=1, keepdims=True) for w in weights]
            for at, (request, head, places, _) in enumerate(items):
                values = [values[slot, :, cols[head]] for _, values, slot in places]
                values = jnp.concatenate(values + [fresh_v[:, cols[head]]], 0)
                num_ref[sz.span(request, head), :] = dot_nn(
                    weights[at].astype(jnp.bfloat16), values
                )
                lane = ((request - first) * sz.kv + head) * 4
                tile = jnp.where(lane_ids == lane, top[at], tile)
                tile = jnp.where(lane_ids == lane + 2, total[at], tile)
        stat_ref[pl.ds(tile_at * sz.rows, sz.rows), :] = tile


def merge_kernel(sz, num_ref, stat_ref, came_ref, out_ref):
    for tile_at, first, last in sz.tiles():
        came_span = pl.ds(sz.all_rows + tile_at * sz.rows, sz.rows)
        mine = stat_ref[pl.ds(tile_at * sz.rows, sz.rows), :]
        came = pair_sums(came_ref[came_span, :].astype(jnp.float32))
        top = jnp.maximum(mine, came)
        keep, add = jnp.exp2((mine - top) * sz.factor), jnp.exp2((came - top) * sz.factor)
        total = mine * pltpu.roll(keep, 2, 1) + came * pltpu.roll(add, 2, 1)
        kind = lax.broadcasted_iota(jnp.int32, top.shape, 1) % 4
        put_stats(sz, out_ref, tile_at, jnp.where(kind == 0, top, total))
        for request in range(first, last):
            for head in range(sz.kv):
                lane = ((request - first) * sz.kv + head) * 4
                span = sz.span(request, head)
                joined = num_ref[span, :] * keep[:, lane : lane + 1]
                joined = joined + came_ref[span, :].astype(jnp.float32) * add[:, lane : lane + 1]
                out_ref[span, :] = joined.astype(jnp.bfloat16)


def join_kernel(sz, num_ref, stat_ref, came_ref, out_ref, out_stat_ref):
    mine = stat_ref[...]
    came = pair_sums(came_ref[sz.all_rows : sz.all_rows + sz.rows, :].astype(jnp.float32))
    top = jnp.maximum(mine, came)
    keep, add = jnp.exp2((mine - top) * sz.factor), jnp.exp2((came - top) * sz.factor)
    total = mine * pltpu.roll(keep, 2, 1) + came * pltpu.roll(add, 2, 1)
    kind = lax.broadcasted_iota(jnp.int32, top.shape, 1) % 4
    out_stat_ref[...] = jnp.where(kind == 0, top, total)
    for request in range(sz.requests):
        for head in range(sz.kv):
            lane = (request * sz.kv + head) * 4
            span = sz.span(request, head)
            joined = num_ref[span, :] * keep[:, lane : lane + 1]
            out_ref[span, :] = joined + came_ref[span, :].astype(jnp.float32) * add[
                :, lane : lane + 1
            ]


def final_kernel(whole, sz, num_ref, stat_ref, *refs):
    *came_refs, out_ref, wide = refs
    lanes = sz.requests * sz.kv * 4
    lane_ids = lax.broadcasted_iota(jnp.int32, (sz.rows, HD), 1)
    mine = stat_ref[...]
    came = jnp.zeros((sz.rows, HD), jnp.float32)
    for chunk, came_ref in enumerate(came_refs):
        tile = pair_sums(came_ref[sz.all_rows : sz.all_rows + sz.rows, :].astype(jnp.float32))
        if chunk:
            tile = pltpu.roll(tile, chunk * lanes, 1)
        came = jnp.where(lane_ids // lanes == chunk, tile, came)
    top = jnp.maximum(mine, came)
    keep, add = jnp.exp2((mine - top) * sz.factor), jnp.exp2((came - top) * sz.factor)
    total = mine * pltpu.roll(keep, 2, 1) + came * pltpu.roll(add, 2, 1)
    total = pltpu.roll(total, HD - 2, 1)
    keep, add = keep / total, add / total
    for row in range(whole.requests):
        chunk, request = row // sz.requests, row % sz.requests
        for head in range(sz.kv):
            lane = (row * sz.kv + head) * 4
            joined = num_ref[whole.span(row, head), :] * keep[:, lane : lane + 1]
            joined = joined + came_refs[chunk][sz.span(request, head), :].astype(
                jnp.float32
            ) * add[:, lane : lane + 1]
            for step in range(sz.steps):
                at = (step * sz.step_rows + head * sz.group) * whole.requests
                wide[pl.ds(at + row, sz.group, stride=whole.requests), :] = joined[
                    step * sz.group : (step + 1) * sz.group
                ]
    for step in range(sz.steps):
        for head in range(sz.step_rows):
            at = (step * sz.step_rows + head) * whole.requests
            out_ref[step, :, head * HD : (head + 1) * HD] = wide[
                at : at + whole.requests, :
            ].astype(jnp.bfloat16)


def fetch_kernel(k_any, v_any, k_ref, v_ref, sems):
    copies = [
        pltpu.make_async_copy(source, target, sems.at[at])
        for at, (source, target) in enumerate(((k_any, k_ref), (v_any, v_ref)))
    ]
    for copy in copies:
        copy.start()
    for copy in copies:
        copy.wait()


def line_shards(
    queries,
    page_keys,
    page_values,
    page_count,
    leaf_keys,
    leaf_values,
    leaf_count,
    new_keys,
    new_values,
    path_owner,
    path_slot,
):
    requests, steps, width = queries.shape
    owners = lax.axis_size("page")
    kv = page_keys.shape[2] // HD
    pages, page_tok = page_keys.shape[:2]
    chunks = 1
    line = (queries, page_keys, page_values, page_count, leaf_keys, leaf_values, leaf_count)
    if requests % chunks or requests * kv * 4 != HD:
        return shards(*line, new_keys, new_values, path_owner, path_slot)
    shape_of = (steps, kv, QH // KVH, path_owner.shape[1], pages, page_tok)
    whole, sz = Sizes(requests, *shape_of), Sizes(requests // chunks, *shape_of)

    def exchange(array, hop):
        return lax.ppermute(array, "page", [(at, at ^ hop) for at in range(owners)])

    def after(array, *others):
        return lax.optimization_barrier((array, *others))[0]

    near, far = CORES, owners - CORES
    smem, vmem, hbm = pltpu.SMEM, pltpu.VMEM, pl.ANY
    shape = jax.ShapeDtypeStruct
    wide = pltpu.VMEM((whole.all_rows, HD), jnp.float32)
    fresh_rows = -(-requests * steps // page_tok) * page_tok
    fresh = pltpu.VMEM((fresh_rows, kv * HD), jnp.bfloat16)
    leaves = pltpu.VMEM((requests, page_tok, kv * HD), jnp.bfloat16)

    def sent(size):
        return (shape((size.all_rows + size.stat_rows, HD), jnp.bfloat16),)

    def exact(size):
        return (
            shape((size.all_rows, HD), jnp.float32),
            shape((size.stat_rows, HD), jnp.float32),
        )

    block = jnp.swapaxes(queries, 0, 1)
    table = jnp.swapaxes(path_owner * pages + path_slot, 0, 1)
    far_q = exchange(block, far)
    near_q = exchange(block, near)
    mate_keys, mate_values, mate_count = (
        exchange(array, 1) for array in (page_keys, page_values, page_count)
    )
    counts = (page_count, mate_count)
    own_pages = plain_call(
        fetch_kernel,
        (shape(page_keys.shape, page_keys.dtype),) * 2,
        [hbm] * 2,
        [pltpu.SemaphoreType.DMA((2,))],
    )(after(page_keys, mate_keys, mate_values, mate_count), page_values)
    all_pages = (*own_pages, mate_keys, mate_values)
    near_table, far_table, cross_table = (exchange(table, hop) for hop in (near, far, near ^ far))
    far_q, near_table, far_table, cross_table = lax.optimization_barrier(
        (far_q, near_table, far_table, cross_table, *all_pages, mate_count)
    )[:4]

    def shared(size, chunk, is_exact, paths, rows):
        return plain_call(
            functools.partial(shared_kernel, size, chunk, is_exact),
            exact(size) if is_exact else sent(size),
            [smem] * 3 + [vmem] * 5,
            [wide],
        )(paths, *counts, rows, *all_pages)

    def merge(part, came):
        return plain_call(functools.partial(merge_kernel, sz), sent(sz), [vmem] * 3)(*part, came)[0]

    cross_q = exchange(far_q, near)
    near_q = after(near_q, far_q)
    far_part = shared(sz, 0, True, far_table, after(far_q, near_q))
    cross_q = after(cross_q, *far_part)
    cross_part = shared(sz, 0, False, cross_table, cross_q)[0]
    cross_back = exchange(cross_part, near)
    near_part = shared(sz, 0, False, near_table, after(near_q, cross_part))[0]
    cross_back = after(cross_back, near_part)
    joined = merge(far_part, cross_back)
    far_back = exchange(joined, far)
    near_back = exchange(after(near_part, joined), near)
    local = plain_call(
        functools.partial(local_kernel, whole, 0),
        exact(whole),
        [smem] * 4 + [vmem] * 5 + [hbm] * 2 + [vmem] * 2,
        [wide, fresh, fresh, leaves, leaves, pltpu.SemaphoreType.DMA((requests, 2))],
    )(
        table,
        *counts,
        leaf_count,
        after(block, joined),
        *all_pages,
        leaf_keys,
        leaf_values,
        jnp.swapaxes(new_keys, 0, 1),
        jnp.swapaxes(new_values, 0, 1),
    )
    state = plain_call(functools.partial(join_kernel, whole), exact(whole), [vmem] * 3)(
        *local, after(near_back, *local)
    )
    (out,) = plain_call(
        functools.partial(final_kernel, whole, sz),
        (shape((steps, requests, width), jnp.bfloat16),),
        [vmem] * 3,
        [wide],
    )(*state, far_back)
    return jnp.swapaxes(out, 0, 1)


def solution(mesh):
    on_line = mesh.shape["sub"] == 1 and mesh.shape["page"] == 4 * CORES
    return jax.shard_map(
        line_shards if on_line else shards,
        mesh=mesh,
        in_specs=(
            P(("groups", "page", "sub"), None, "head"),
            P(("groups", "page"), None, "head"),
            P(("groups", "page"), None, "head"),
            P(("groups", "page")),
            P(("groups", "page", "sub"), None, "head"),
            P(("groups", "page", "sub"), None, "head"),
            P(("groups", "page", "sub")),
            P(("groups", "page", "sub"), None, "head"),
            P(("groups", "page", "sub"), None, "head"),
            P(("groups", "page", "sub"), None),
            P(("groups", "page", "sub"), None),
        ),
        out_specs=P(("groups", "page", "sub"), None, "head"),
        check_vma=False,
    )
```

```python
import functools
import math

import jax
import jax.numpy as jnp
from jax import lax
from jax.experimental import pallas as pl
from jax.experimental.pallas import tpu as pltpu
from jax.sharding import PartitionSpec as P

HD = 128
QH = 128
KVH = 8


def page_states(query_rows, keys, values, counts):
    slot_rows = query_rows.shape[0]
    kv_local = keys.shape[2] // HD
    group_size = QH // KVH
    step_count = query_rows.shape[1] // (kv_local * group_size * HD)
    page_tok = keys.shape[1]
    query_five = query_rows.reshape(slot_rows, step_count, kv_local, group_size, HD)
    key_heads = keys.reshape(slot_rows, page_tok, kv_local, HD)
    value_heads = values.reshape(slot_rows, page_tok, kv_local, HD)
    scores = jnp.einsum(
        "nskgd,ntkd->nskgt", query_five, key_heads, preferred_element_type=jnp.float32
    ) * (1.0 / math.sqrt(HD))
    allowed = jnp.arange(page_tok, dtype=jnp.int32)[None, :] < counts[:, None]
    scores = jnp.where(allowed[:, None, None, None, :], scores, -jnp.inf)
    item_max = jnp.max(scores, axis=-1)
    weights = jnp.exp(scores - item_max[..., None])
    item_total = jnp.sum(weights, axis=-1)
    mixed = jnp.einsum(
        "nskgt,ntkd->nskgd",
        weights.astype(jnp.bfloat16),
        value_heads,
        preferred_element_type=jnp.float32,
    )
    item_out = (mixed / item_total[..., None]).astype(jnp.bfloat16)
    return (
        item_out.reshape(slot_rows, -1),
        item_max.reshape(slot_rows, -1),
        item_total.reshape(slot_rows, -1),
    )


def in_blocks(step_fn, arrays, rows_per_slot):
    owner_count = arrays[0].shape[0]
    slot_width = arrays[0].shape[1]
    wanted_slots = -(-512 // max(1, slot_width * rows_per_slot))
    divisors = [
        candidate
        for candidate in range(1, owner_count + 1)
        if owner_count % candidate == 0 and candidate >= wanted_slots
    ]
    merge_count = min(divisors)
    merged = tuple(
        (
            member.reshape(
                (owner_count // merge_count, merge_count * slot_width) + member.shape[2:]
            )
            for member in arrays
        )
    )
    results = lax.map(step_fn, merged)
    return tuple(
        (member.reshape((owner_count, slot_width) + member.shape[2:]) for member in results)
    )


def shards(
    queries,
    page_keys,
    page_values,
    page_count,
    leaf_keys,
    leaf_values,
    leaf_count,
    new_keys,
    new_values,
    path_owner,
    path_slot,
):
    request_rows, step_count, head_width = queries.shape
    kv_local = page_keys.shape[2] // HD
    group_size = QH // KVH
    page_tok = page_keys.shape[1]
    level_count = path_owner.shape[1]
    owner_count = lax.axis_size("page")
    capacity = max(
        2, min(request_rows, (2 * request_rows * level_count + owner_count - 1) // owner_count)
    )
    score_scale = 1.0 / math.sqrt(HD)
    rows_per_slot = step_count * kv_local * group_size
    item_count = request_rows * level_count
    slot_count = owner_count * capacity
    flat_owner = path_owner.reshape(item_count)
    flat_slot = path_slot.reshape(item_count)
    owner_hot = (flat_owner[:, None] == jnp.arange(owner_count, dtype=jnp.int32)[None, :]).astype(
        jnp.int32
    )
    earlier = jnp.cumsum(owner_hot, axis=0) - owner_hot
    owner_rank = jnp.sum(earlier * owner_hot, axis=1)
    position = flat_owner * capacity + owner_rank
    slot_match = (position[None, :] == jnp.arange(slot_count, dtype=jnp.int32)[:, None]).astype(
        jnp.int32
    )
    item_of_slot = jnp.sum(slot_match * jnp.arange(item_count, dtype=jnp.int32)[None, :], axis=1)
    slot_used = jnp.sum(slot_match, axis=1) > 0
    page_ids = jnp.where(slot_used, jnp.take(flat_slot, item_of_slot, axis=0), 0).reshape(
        owner_count, capacity
    )
    outgoing = jnp.take(queries, item_of_slot // level_count, axis=0).reshape(
        owner_count, capacity, step_count * head_width
    )

    def remote_block(packed):
        block_ids = packed[1]
        return page_states(
            packed[0],
            jnp.take(page_keys, block_ids, axis=0),
            jnp.take(page_values, block_ids, axis=0),
            jnp.take(page_count, block_ids, axis=0),
        )

    states = in_blocks(
        remote_block,
        (
            lax.all_to_all(outgoing, "page", split_axis=0, concat_axis=0, tiled=True),
            lax.all_to_all(page_ids, "page", split_axis=0, concat_axis=0, tiled=True),
        ),
        rows_per_slot,
    )
    out_back = lax.all_to_all(states[0], "page", split_axis=0, concat_axis=0, tiled=True)
    max_back = lax.all_to_all(states[1], "page", split_axis=0, concat_axis=0, tiled=True)
    total_back = lax.all_to_all(states[2], "page", split_axis=0, concat_axis=0, tiled=True)
    item_out = jnp.take(out_back.reshape(slot_count, step_count * head_width), position, axis=0)
    item_out = item_out.astype(jnp.float32).reshape(
        request_rows, level_count, step_count, kv_local, group_size, HD
    )
    item_max = jnp.take(max_back.reshape(slot_count, rows_per_slot), position, axis=0)
    item_max = item_max.reshape(request_rows, level_count, step_count, kv_local, group_size)
    item_total = jnp.take(total_back.reshape(slot_count, rows_per_slot), position, axis=0)
    item_total = item_total.reshape(request_rows, level_count, step_count, kv_local, group_size)
    query_five = queries.reshape(request_rows, step_count, kv_local, group_size, HD)
    leaf_heads = leaf_keys.reshape(request_rows, page_tok, kv_local, HD)
    leaf_value_heads = leaf_values.reshape(request_rows, page_tok, kv_local, HD)
    fresh_heads = new_keys.reshape(request_rows, step_count, kv_local, HD)
    fresh_value_heads = new_values.reshape(request_rows, step_count, kv_local, HD)
    leaf_scores = (
        jnp.einsum("rskgd,rtkd->rskgt", query_five, leaf_heads, preferred_element_type=jnp.float32)
        * score_scale
    )
    leaf_allowed = jnp.arange(page_tok, dtype=jnp.int32)[None, :] < leaf_count[:, None]
    leaf_scores = jnp.where(leaf_allowed[:, None, None, None, :], leaf_scores, -jnp.inf)
    fresh_scores = (
        jnp.einsum("rskgd,rukd->rskgu", query_five, fresh_heads, preferred_element_type=jnp.float32)
        * score_scale
    )
    causal = (
        jnp.arange(step_count, dtype=jnp.int32)[None, :]
        <= jnp.arange(step_count, dtype=jnp.int32)[:, None]
    )
    fresh_scores = jnp.where(causal[None, :, None, None, :], fresh_scores, -jnp.inf)
    local_max = jnp.maximum(jnp.max(leaf_scores, axis=-1), jnp.max(fresh_scores, axis=-1))
    leaf_weights = jnp.exp(leaf_scores - local_max[..., None])
    fresh_weights = jnp.exp(fresh_scores - local_max[..., None])
    local_total = jnp.sum(leaf_weights, axis=-1) + jnp.sum(fresh_weights, axis=-1)
    local_sum = jnp.einsum(
        "rskgt,rtkd->rskgd",
        leaf_weights.astype(jnp.bfloat16),
        leaf_value_heads,
        preferred_element_type=jnp.float32,
    )
    local_sum = local_sum + jnp.einsum(
        "rskgu,rukd->rskgd",
        fresh_weights.astype(jnp.bfloat16),
        fresh_value_heads,
        preferred_element_type=jnp.float32,
    )
    local_out = local_sum / local_total[..., None]
    top_score = jnp.maximum(local_max, jnp.max(item_max, axis=1))
    local_mass = local_total * jnp.exp(local_max - top_score)
    item_mass = item_total * jnp.exp(item_max - top_score[:, None])
    numerator = local_mass[..., None] * local_out + jnp.sum(item_mass[..., None] * item_out, axis=1)
    denominator = local_mass + jnp.sum(item_mass, axis=1)
    return (
        (numerator / denominator[..., None])
        .astype(jnp.bfloat16)
        .reshape(request_rows, step_count, head_width)
    )


NEG = -(2.0**127)
CORES = 2


def pair_sums(tile):
    return tile + pltpu.roll(tile, tile.shape[1] - 1, 1)


def two_pieces(values):
    high = values.astype(jnp.bfloat16).astype(jnp.float32)
    low = (values - high).astype(jnp.bfloat16).astype(jnp.float32)
    return high, low


def dot_nt(a, b):
    return lax.dot_general(a, b, (((1,), (1,)), ((), ())), preferred_element_type=jnp.float32)


def dot_nn(a, b):
    return lax.dot_general(a, b, (((1,), (0,)), ((), ())), preferred_element_type=jnp.float32)


def plain_call(kernel, out_shape, in_memory, scratch=(), flops=0, num_bytes=0):
    return pl.pallas_call(
        kernel,
        out_shape=out_shape,
        in_specs=[pl.BlockSpec(memory_space=space) for space in in_memory],
        out_specs=tuple(pl.BlockSpec(memory_space=pltpu.VMEM) for _ in out_shape),
        scratch_shapes=list(scratch),
        compiler_params=pltpu.CompilerParams(vmem_limit_bytes=16 * 1024 * 1024),
        cost_estimate=pl.CostEstimate(flops=flops, bytes_accessed=num_bytes, transcendentals=0),
    )


class Sizes:
    def __init__(self, requests, steps, kv, group, levels, pages, page_tok):
        self.requests, self.steps, self.kv, self.group = requests, steps, kv, group
        self.levels, self.pages, self.page_tok = levels, pages, page_tok
        self.rows = steps * group
        self.step_rows = kv * group
        self.all_rows = requests * kv * self.rows
        self.per_tile = HD // (4 * kv)
        self.tile_count = -(-requests // self.per_tile)
        self.stat_rows = self.tile_count * self.rows
        self.factor = 1.0 / math.sqrt(HD) * math.log2(math.e)

    def tiles(self):
        for tile_at in range(self.tile_count):
            first = tile_at * self.per_tile
            yield tile_at, first, min(self.requests, first + self.per_tile)

    def spread(self, q_ref, wide):
        for step in range(self.steps):
            for head in range(self.step_rows):
                at = (step * self.step_rows + head) * self.requests
                wide[at : at + self.requests, :] = q_ref[
                    step, :, head * HD : (head + 1) * HD
                ].astype(jnp.float32)

    def pick(self, wide, request, kv_head):
        parts = []
        for step in range(self.steps):
            at = (step * self.step_rows + kv_head * self.group) * self.requests
            parts.append(wide[pl.ds(at + request, self.group, stride=self.requests), :])
        return jnp.concatenate(parts, axis=0).astype(jnp.bfloat16)

    def span(self, request, kv_head):
        at = (request * self.kv + kv_head) * self.rows
        return pl.ds(at if isinstance(at, int) else pl.multiple_of(at, 16), self.rows)

    def find(self, table_ref, count_ref, owner, request):
        slot, used = jnp.int32(0), jnp.int32(0)
        for level in range(self.levels):
            index = table_ref[level, request]
            hit = index // self.pages == owner
            slot = jnp.where(hit, index % self.pages, slot)
            used = jnp.where(hit, 1, used)
        return slot, used * count_ref[slot]


def shared_kernel(
    sz, chunk, exact, table_ref, count0_ref, count1_ref, q_ref, k0, v0, k1, v1, *rest
):
    *outs, wide = rest
    num_ref = outs[0]
    me = lax.axis_index("page")
    mate = jnp.bitwise_xor(me, 1)
    lane_ids = lax.broadcasted_iota(jnp.int32, (sz.rows, HD), 1)
    token_ids = lax.broadcasted_iota(jnp.int32, (sz.rows, sz.page_tok), 1)
    heads = range(sz.kv)
    sz.spread(q_ref, wide)
    for tile_at, first, last in sz.tiles():
        tile = jnp.zeros((sz.rows, HD), jnp.float32)
        for start in range(first, last, 4):
            items = []
            for request in range(start, min(last, start + 4)):
                slot0, count0 = sz.find(table_ref, count0_ref, me, request)
                slot1, count1 = sz.find(table_ref, count1_ref, mate, request)
                allowed = jnp.concatenate([token_ids < count0, token_ids < count1], axis=1)
                items += [(request, head, slot0, slot1, allowed) for head in heads]
            scores = []
            for request, head, slot0, slot1, allowed in items:
                cols = slice(head * HD, (head + 1) * HD)
                keys = jnp.concatenate([k0[slot0, :, cols], k1[slot1, :, cols]], 0)
                s = dot_nt(sz.pick(wide, request, head), keys)
                scores.append(jnp.where(allowed, s, NEG))
            point = [sum(two_pieces(jnp.max(s, axis=1, keepdims=True))) for s in scores]
            weights = [jnp.exp2((s - p) * sz.factor) for s, p in zip(scores, point)]
            total = [jnp.sum(w, axis=1, keepdims=True) for w in weights]
            for at, (request, head, slot0, slot1, _) in enumerate(items):
                cols = slice(head * HD, (head + 1) * HD)
                values = jnp.concatenate([v0[slot0, :, cols], v1[slot1, :, cols]], 0)
                num = dot_nn(weights[at].astype(jnp.bfloat16), values)
                num_ref[sz.span(request, head), :] = num.astype(num_ref.dtype)
                lane = ((request - first) * sz.kv + head) * 4
                tile = jnp.where(lane_ids == lane, point[at], tile)
                tile = jnp.where(lane_ids == lane + 2, total[at], tile)
        if exact:
            outs[1][pl.ds(tile_at * sz.rows, sz.rows), :] = tile
        else:
            put_stats(sz, num_ref, tile_at, tile)


def put_stats(sz, out_ref, tile_at, tile):
    kind = lax.broadcasted_iota(jnp.int32, tile.shape, 1) % 4
    high, low = two_pieces(tile)
    tile = jnp.where(kind % 2 == 0, high, pltpu.roll(low, 1, 1))
    out_ref[pl.ds(sz.all_rows + tile_at * sz.rows, sz.rows), :] = tile.astype(jnp.bfloat16)


def local_kernel(
    sz,
    chunk,
    table_ref,
    count0_ref,
    count1_ref,
    leaf_count_ref,
    q_ref,
    k0,
    v0,
    k1,
    v1,
    leaf_k_any,
    leaf_v_any,
    new_k,
    new_v,
    num_ref,
    stat_ref,
    wide,
    fresh_k,
    fresh_v,
    leaf_k,
    leaf_v,
    leaf_sem,
):
    def leaf_copy(request, whole, part, sem_at):
        return pltpu.make_async_copy(
            whole.at[chunk * sz.requests + request], part.at[request], leaf_sem.at[request, sem_at]
        )

    for request in range(sz.requests):
        leaf_copy(request, leaf_k_any, leaf_k, 0).start()
        leaf_copy(request, leaf_v_any, leaf_v, 1).start()
    me = lax.axis_index("page")
    mate = jnp.bitwise_xor(me, 1)
    lane_ids = lax.broadcasted_iota(jnp.int32, (sz.rows, HD), 1)
    token_ids = lax.broadcasted_iota(jnp.int32, (sz.rows, sz.page_tok), 1)
    fresh = fresh_k.shape[0]
    fresh_ids = lax.broadcasted_iota(jnp.int32, (sz.rows, fresh), 1)
    step_ids = lax.broadcasted_iota(jnp.int32, (sz.rows, fresh), 0) // sz.group
    device_requests = new_k.shape[1]
    causal = (fresh_ids // device_requests) <= step_ids
    fresh_request = fresh_ids % device_requests
    heads = range(sz.kv)
    cols = [slice(head * HD, (head + 1) * HD) for head in heads]
    sz.spread(q_ref, wide)
    for new_ref, full in ((new_k, fresh_k), (new_v, fresh_v)):
        rows = [new_ref[step].astype(jnp.float32) for step in range(sz.steps)]
        filler = fresh - sz.steps * device_requests
        if filler:
            rows.append(jnp.zeros((filler, sz.kv * HD), jnp.float32))
        full[...] = jnp.concatenate(rows, axis=0).astype(full.dtype)
    for tile_at, first, last in sz.tiles():
        tile = jnp.zeros((sz.rows, HD), jnp.float32)
        for start in range(first, last, 2):
            items = []
            for request in range(start, min(last, start + 2)):
                row = chunk * sz.requests + request
                slot0, count0 = sz.find(table_ref, count0_ref, me, row)
                slot1, count1 = sz.find(table_ref, count1_ref, mate, row)
                allowed = (
                    token_ids < count0,
                    token_ids < count1,
                    token_ids < leaf_count_ref[row],
                    causal & (fresh_request == row),
                )
                allowed = jnp.concatenate(allowed, axis=1)
                places = ((k0, v0, slot0), (k1, v1, slot1), (leaf_k, leaf_v, request))
                items += [(request, head, places, allowed) for head in heads]
                leaf_copy(request, leaf_k_any, leaf_k, 0).wait()
                leaf_copy(request, leaf_v_any, leaf_v, 1).wait()
            scores = []
            for request, head, places, allowed in items:
                keys = [keys[at, :, cols[head]] for keys, _, at in places]
                keys = jnp.concatenate(keys + [fresh_k[:, cols[head]]], 0)
                s = dot_nt(sz.pick(wide, request, head), keys)
                scores.append(jnp.where(allowed, s, NEG))
            top = [jnp.max(s, axis=1, keepdims=True) for s in scores]
            weights = [jnp.exp2((s - t) * sz.factor) for s, t in zip(scores, top)]
            total = [jnp.sum(w, axis=1, keepdims=True) for w in weights]
            for at, (request, head, places, _) in enumerate(items):
                values = [values[slot, :, cols[head]] for _, values, slot in places]
                values = jnp.concatenate(values + [fresh_v[:, cols[head]]], 0)
                num_ref[sz.span(request, head), :] = dot_nn(
                    weights[at].astype(jnp.bfloat16), values
                )
                lane = ((request - first) * sz.kv + head) * 4
                tile = jnp.where(lane_ids == lane, top[at], tile)
                tile = jnp.where(lane_ids == lane + 2, total[at], tile)
        stat_ref[pl.ds(tile_at * sz.rows, sz.rows), :] = tile


def merge_kernel(sz, num_ref, stat_ref, came_ref, out_ref):
    for tile_at, first, last in sz.tiles():
        came_span = pl.ds(sz.all_rows + tile_at * sz.rows, sz.rows)
        mine = stat_ref[pl.ds(tile_at * sz.rows, sz.rows), :]
        came = pair_sums(came_ref[came_span, :].astype(jnp.float32))
        top = jnp.maximum(mine, came)
        keep, add = jnp.exp2((mine - top) * sz.factor), jnp.exp2((came - top) * sz.factor)
        total = mine * pltpu.roll(keep, 2, 1) + came * pltpu.roll(add, 2, 1)
        kind = lax.broadcasted_iota(jnp.int32, top.shape, 1) % 4
        put_stats(sz, out_ref, tile_at, jnp.where(kind == 0, top, total))
        for request in range(first, last):
            for head in range(sz.kv):
                lane = ((request - first) * sz.kv + head) * 4
                span = sz.span(request, head)
                joined = num_ref[span, :] * keep[:, lane : lane + 1]
                joined = joined + came_ref[span, :].astype(jnp.float32) * add[:, lane : lane + 1]
                out_ref[span, :] = joined.astype(jnp.bfloat16)


def join_kernel(sz, num_ref, stat_ref, came_ref, out_ref, out_stat_ref):
    mine = stat_ref[...]
    came = pair_sums(came_ref[sz.all_rows : sz.all_rows + sz.rows, :].astype(jnp.float32))
    top = jnp.maximum(mine, came)
    keep, add = jnp.exp2((mine - top) * sz.factor), jnp.exp2((came - top) * sz.factor)
    total = mine * pltpu.roll(keep, 2, 1) + came * pltpu.roll(add, 2, 1)
    kind = lax.broadcasted_iota(jnp.int32, top.shape, 1) % 4
    out_stat_ref[...] = jnp.where(kind == 0, top, total)
    for request in range(sz.requests):
        for head in range(sz.kv):
            lane = (request * sz.kv + head) * 4
            span = sz.span(request, head)
            joined = num_ref[span, :] * keep[:, lane : lane + 1]
            out_ref[span, :] = joined + came_ref[span, :].astype(jnp.float32) * add[
                :, lane : lane + 1
            ]


def final_kernel(whole, sz, num_ref, stat_ref, *refs):
    *came_refs, out_ref, wide = refs
    lanes = sz.requests * sz.kv * 4
    lane_ids = lax.broadcasted_iota(jnp.int32, (sz.rows, HD), 1)
    mine = stat_ref[...]
    came = jnp.zeros((sz.rows, HD), jnp.float32)
    for chunk, came_ref in enumerate(came_refs):
        tile = pair_sums(came_ref[sz.all_rows : sz.all_rows + sz.rows, :].astype(jnp.float32))
        if chunk:
            tile = pltpu.roll(tile, chunk * lanes, 1)
        came = jnp.where(lane_ids // lanes == chunk, tile, came)
    top = jnp.maximum(mine, came)
    keep, add = jnp.exp2((mine - top) * sz.factor), jnp.exp2((came - top) * sz.factor)
    total = mine * pltpu.roll(keep, 2, 1) + came * pltpu.roll(add, 2, 1)
    total = pltpu.roll(total, HD - 2, 1)
    keep, add = keep / total, add / total
    for row in range(whole.requests):
        chunk, request = row // sz.requests, row % sz.requests
        for head in range(sz.kv):
            lane = (row * sz.kv + head) * 4
            joined = num_ref[whole.span(row, head), :] * keep[:, lane : lane + 1]
            joined = joined + came_refs[chunk][sz.span(request, head), :].astype(
                jnp.float32
            ) * add[:, lane : lane + 1]
            for step in range(sz.steps):
                at = (step * sz.step_rows + head * sz.group) * whole.requests
                wide[pl.ds(at + row, sz.group, stride=whole.requests), :] = joined[
                    step * sz.group : (step + 1) * sz.group
                ]
    for step in range(sz.steps):
        for head in range(sz.step_rows):
            at = (step * sz.step_rows + head) * whole.requests
            out_ref[step, :, head * HD : (head + 1) * HD] = wide[
                at : at + whole.requests, :
            ].astype(jnp.bfloat16)


def fetch_kernel(k_any, v_any, k_ref, v_ref, sems):
    copies = [
        pltpu.make_async_copy(source, target, sems.at[at])
        for at, (source, target) in enumerate(((k_any, k_ref), (v_any, v_ref)))
    ]
    for copy in copies:
        copy.start()
    for copy in copies:
        copy.wait()


def line_shards(
    queries,
    page_keys,
    page_values,
    page_count,
    leaf_keys,
    leaf_values,
    leaf_count,
    new_keys,
    new_values,
    path_owner,
    path_slot,
):
    requests, steps, width = queries.shape
    owners = lax.axis_size("page")
    kv = page_keys.shape[2] // HD
    pages, page_tok = page_keys.shape[:2]
    chunks = 1
    line = (queries, page_keys, page_values, page_count, leaf_keys, leaf_values, leaf_count)
    if requests % chunks or requests * kv * 4 != HD:
        return shards(*line, new_keys, new_values, path_owner, path_slot)
    shape_of = (steps, kv, QH // KVH, path_owner.shape[1], pages, page_tok)
    whole, sz = Sizes(requests, *shape_of), Sizes(requests // chunks, *shape_of)

    def exchange(array, hop):
        return lax.ppermute(array, "page", [(at, at ^ hop) for at in range(owners)])

    def after(array, *others):
        return lax.optimization_barrier((array, *others))[0]

    near, far = CORES, owners - CORES
    smem, vmem, hbm = pltpu.SMEM, pltpu.VMEM, pl.ANY
    shape = jax.ShapeDtypeStruct
    wide = pltpu.VMEM((whole.all_rows + requests, HD), jnp.float32)
    fresh_rows = -(-requests * steps // page_tok) * page_tok
    fresh = pltpu.VMEM((fresh_rows, kv * HD), jnp.bfloat16)
    leaves = pltpu.VMEM((requests, page_tok, kv * HD), jnp.bfloat16)

    def sent(size):
        return (shape((size.all_rows + size.stat_rows, HD), jnp.bfloat16),)

    def exact(size):
        return (
            shape((size.all_rows, HD), jnp.float32),
            shape((size.stat_rows, HD), jnp.float32),
        )

    block = jnp.swapaxes(queries, 0, 1)
    table = jnp.swapaxes(path_owner * pages + path_slot, 0, 1)
    far_q = exchange(block, far)
    near_q = exchange(block, near)
    mate_keys, mate_values, mate_count = (
        exchange(array, 1) for array in (page_keys, page_values, page_count)
    )
    counts = (page_count, mate_count)
    own_pages = plain_call(
        fetch_kernel,
        (shape(page_keys.shape, page_keys.dtype),) * 2,
        [hbm] * 2,
        [pltpu.SemaphoreType.DMA((2,))],
    )(after(page_keys, mate_keys, mate_values, mate_count), page_values)
    all_pages = (*own_pages, mate_keys, mate_values)
    near_table, far_table, cross_table = (exchange(table, hop) for hop in (near, far, near ^ far))
    far_q, near_table, far_table, cross_table = lax.optimization_barrier(
        (far_q, near_table, far_table, cross_table, *all_pages, mate_count)
    )[:4]

    def shared(size, chunk, is_exact, paths, rows):
        return plain_call(
            functools.partial(shared_kernel, size, chunk, is_exact),
            exact(size) if is_exact else sent(size),
            [smem] * 3 + [vmem] * 5,
            [wide],
        )(paths, *counts, rows, *all_pages)

    def merge(part, came):
        return plain_call(functools.partial(merge_kernel, sz), sent(sz), [vmem] * 3)(*part, came)[0]

    cross_q = exchange(far_q, near)
    near_q = after(near_q, far_q)
    far_part = shared(sz, 0, True, far_table, after(far_q, near_q))
    cross_q = after(cross_q, *far_part)
    cross_part = shared(sz, 0, False, cross_table, cross_q)[0]
    cross_back = exchange(cross_part, near)
    near_part = shared(sz, 0, False, near_table, after(near_q, cross_part))[0]
    cross_back = after(cross_back, near_part)
    joined = merge(far_part, cross_back)
    far_back = exchange(joined, far)
    near_back = exchange(after(near_part, joined), near)
    local = plain_call(
        functools.partial(local_kernel, whole, 0),
        exact(whole),
        [smem] * 4 + [vmem] * 5 + [hbm] * 2 + [vmem] * 2,
        [wide, fresh, fresh, leaves, leaves, pltpu.SemaphoreType.DMA((requests, 2))],
    )(
        table,
        *counts,
        leaf_count,
        after(block, joined),
        *all_pages,
        leaf_keys,
        leaf_values,
        jnp.swapaxes(new_keys, 0, 1),
        jnp.swapaxes(new_values, 0, 1),
    )
    state = plain_call(functools.partial(join_kernel, whole), exact(whole), [vmem] * 3)(
        *local, after(near_back, *local)
    )
    (out,) = plain_call(
        functools.partial(final_kernel, whole, sz),
        (shape((steps, requests, width), jnp.bfloat16),),
        [vmem] * 3,
        [wide],
    )(*state, far_back)
    return jnp.swapaxes(out, 0, 1)


def solution(mesh):
    on_line = mesh.shape["sub"] == 1 and mesh.shape["page"] == 4 * CORES
    return jax.shard_map(
        line_shards if on_line else shards,
        mesh=mesh,
        in_specs=(
            P(("groups", "page", "sub"), None, "head"),
            P(("groups", "page"), None, "head"),
            P(("groups", "page"), None, "head"),
            P(("groups", "page")),
            P(("groups", "page", "sub"), None, "head"),
            P(("groups", "page", "sub"), None, "head"),
            P(("groups", "page", "sub")),
            P(("groups", "page", "sub"), None, "head"),
            P(("groups", "page", "sub"), None, "head"),
            P(("groups", "page", "sub"), None),
            P(("groups", "page", "sub"), None),
        ),
        out_specs=P(("groups", "page", "sub"), None, "head"),
        check_vma=False,
    )
```

```python
import functools
import math

import jax
import jax.numpy as jnp
from jax import lax
from jax.experimental import pallas as pl
from jax.experimental.pallas import tpu as pltpu
from jax.sharding import PartitionSpec as P

HD = 128
QH = 128
KVH = 8


def page_states(query_rows, keys, values, counts):
    slot_rows = query_rows.shape[0]
    kv_local = keys.shape[2] // HD
    group_size = QH // KVH
    step_count = query_rows.shape[1] // (kv_local * group_size * HD)
    page_tok = keys.shape[1]
    query_five = query_rows.reshape(slot_rows, step_count, kv_local, group_size, HD)
    key_heads = keys.reshape(slot_rows, page_tok, kv_local, HD)
    value_heads = values.reshape(slot_rows, page_tok, kv_local, HD)
    scores = jnp.einsum(
        "nskgd,ntkd->nskgt", query_five, key_heads, preferred_element_type=jnp.float32
    ) * (1.0 / math.sqrt(HD))
    allowed = jnp.arange(page_tok, dtype=jnp.int32)[None, :] < counts[:, None]
    scores = jnp.where(allowed[:, None, None, None, :], scores, -jnp.inf)
    item_max = jnp.max(scores, axis=-1)
    weights = jnp.exp(scores - item_max[..., None])
    item_total = jnp.sum(weights, axis=-1)
    mixed = jnp.einsum(
        "nskgt,ntkd->nskgd",
        weights.astype(jnp.bfloat16),
        value_heads,
        preferred_element_type=jnp.float32,
    )
    item_out = (mixed / item_total[..., None]).astype(jnp.bfloat16)
    return (
        item_out.reshape(slot_rows, -1),
        item_max.reshape(slot_rows, -1),
        item_total.reshape(slot_rows, -1),
    )


def in_blocks(step_fn, arrays, rows_per_slot):
    owner_count = arrays[0].shape[0]
    slot_width = arrays[0].shape[1]
    wanted_slots = -(-512 // max(1, slot_width * rows_per_slot))
    divisors = [
        candidate
        for candidate in range(1, owner_count + 1)
        if owner_count % candidate == 0 and candidate >= wanted_slots
    ]
    merge_count = min(divisors)
    merged = tuple(
        (
            member.reshape(
                (owner_count // merge_count, merge_count * slot_width) + member.shape[2:]
            )
            for member in arrays
        )
    )
    results = lax.map(step_fn, merged)
    return tuple(
        (member.reshape((owner_count, slot_width) + member.shape[2:]) for member in results)
    )


def shards(
    queries,
    page_keys,
    page_values,
    page_count,
    leaf_keys,
    leaf_values,
    leaf_count,
    new_keys,
    new_values,
    path_owner,
    path_slot,
):
    request_rows, step_count, head_width = queries.shape
    kv_local = page_keys.shape[2] // HD
    group_size = QH // KVH
    page_tok = page_keys.shape[1]
    level_count = path_owner.shape[1]
    owner_count = lax.axis_size("page")
    capacity = max(
        2, min(request_rows, (2 * request_rows * level_count + owner_count - 1) // owner_count)
    )
    score_scale = 1.0 / math.sqrt(HD)
    rows_per_slot = step_count * kv_local * group_size
    item_count = request_rows * level_count
    slot_count = owner_count * capacity
    flat_owner = path_owner.reshape(item_count)
    flat_slot = path_slot.reshape(item_count)
    owner_hot = (flat_owner[:, None] == jnp.arange(owner_count, dtype=jnp.int32)[None, :]).astype(
        jnp.int32
    )
    earlier = jnp.cumsum(owner_hot, axis=0) - owner_hot
    owner_rank = jnp.sum(earlier * owner_hot, axis=1)
    position = flat_owner * capacity + owner_rank
    slot_match = (position[None, :] == jnp.arange(slot_count, dtype=jnp.int32)[:, None]).astype(
        jnp.int32
    )
    item_of_slot = jnp.sum(slot_match * jnp.arange(item_count, dtype=jnp.int32)[None, :], axis=1)
    slot_used = jnp.sum(slot_match, axis=1) > 0
    page_ids = jnp.where(slot_used, jnp.take(flat_slot, item_of_slot, axis=0), 0).reshape(
        owner_count, capacity
    )
    outgoing = jnp.take(queries, item_of_slot // level_count, axis=0).reshape(
        owner_count, capacity, step_count * head_width
    )

    def remote_block(packed):
        block_ids = packed[1]
        return page_states(
            packed[0],
            jnp.take(page_keys, block_ids, axis=0),
            jnp.take(page_values, block_ids, axis=0),
            jnp.take(page_count, block_ids, axis=0),
        )

    states = in_blocks(
        remote_block,
        (
            lax.all_to_all(outgoing, "page", split_axis=0, concat_axis=0, tiled=True),
            lax.all_to_all(page_ids, "page", split_axis=0, concat_axis=0, tiled=True),
        ),
        rows_per_slot,
    )
    out_back = lax.all_to_all(states[0], "page", split_axis=0, concat_axis=0, tiled=True)
    max_back = lax.all_to_all(states[1], "page", split_axis=0, concat_axis=0, tiled=True)
    total_back = lax.all_to_all(states[2], "page", split_axis=0, concat_axis=0, tiled=True)
    item_out = jnp.take(out_back.reshape(slot_count, step_count * head_width), position, axis=0)
    item_out = item_out.astype(jnp.float32).reshape(
        request_rows, level_count, step_count, kv_local, group_size, HD
    )
    item_max = jnp.take(max_back.reshape(slot_count, rows_per_slot), position, axis=0)
    item_max = item_max.reshape(request_rows, level_count, step_count, kv_local, group_size)
    item_total = jnp.take(total_back.reshape(slot_count, rows_per_slot), position, axis=0)
    item_total = item_total.reshape(request_rows, level_count, step_count, kv_local, group_size)
    query_five = queries.reshape(request_rows, step_count, kv_local, group_size, HD)
    leaf_heads = leaf_keys.reshape(request_rows, page_tok, kv_local, HD)
    leaf_value_heads = leaf_values.reshape(request_rows, page_tok, kv_local, HD)
    fresh_heads = new_keys.reshape(request_rows, step_count, kv_local, HD)
    fresh_value_heads = new_values.reshape(request_rows, step_count, kv_local, HD)
    leaf_scores = (
        jnp.einsum("rskgd,rtkd->rskgt", query_five, leaf_heads, preferred_element_type=jnp.float32)
        * score_scale
    )
    leaf_allowed = jnp.arange(page_tok, dtype=jnp.int32)[None, :] < leaf_count[:, None]
    leaf_scores = jnp.where(leaf_allowed[:, None, None, None, :], leaf_scores, -jnp.inf)
    fresh_scores = (
        jnp.einsum("rskgd,rukd->rskgu", query_five, fresh_heads, preferred_element_type=jnp.float32)
        * score_scale
    )
    causal = (
        jnp.arange(step_count, dtype=jnp.int32)[None, :]
        <= jnp.arange(step_count, dtype=jnp.int32)[:, None]
    )
    fresh_scores = jnp.where(causal[None, :, None, None, :], fresh_scores, -jnp.inf)
    local_max = jnp.maximum(jnp.max(leaf_scores, axis=-1), jnp.max(fresh_scores, axis=-1))
    leaf_weights = jnp.exp(leaf_scores - local_max[..., None])
    fresh_weights = jnp.exp(fresh_scores - local_max[..., None])
    local_total = jnp.sum(leaf_weights, axis=-1) + jnp.sum(fresh_weights, axis=-1)
    local_sum = jnp.einsum(
        "rskgt,rtkd->rskgd",
        leaf_weights.astype(jnp.bfloat16),
        leaf_value_heads,
        preferred_element_type=jnp.float32,
    )
    local_sum = local_sum + jnp.einsum(
        "rskgu,rukd->rskgd",
        fresh_weights.astype(jnp.bfloat16),
        fresh_value_heads,
        preferred_element_type=jnp.float32,
    )
    local_out = local_sum / local_total[..., None]
    top_score = jnp.maximum(local_max, jnp.max(item_max, axis=1))
    local_mass = local_total * jnp.exp(local_max - top_score)
    item_mass = item_total * jnp.exp(item_max - top_score[:, None])
    numerator = local_mass[..., None] * local_out + jnp.sum(item_mass[..., None] * item_out, axis=1)
    denominator = local_mass + jnp.sum(item_mass, axis=1)
    return (
        (numerator / denominator[..., None])
        .astype(jnp.bfloat16)
        .reshape(request_rows, step_count, head_width)
    )


NEG = -(2.0**127)
CORES = 2


def pair_sums(tile):
    return tile + pltpu.roll(tile, tile.shape[1] - 1, 1)


def two_pieces(values):
    high = values.astype(jnp.bfloat16).astype(jnp.float32)
    low = (values - high).astype(jnp.bfloat16).astype(jnp.float32)
    return high, low


def dot_nt(a, b):
    return lax.dot_general(a, b, (((1,), (1,)), ((), ())), preferred_element_type=jnp.float32)


def dot_nn(a, b):
    return lax.dot_general(a, b, (((1,), (0,)), ((), ())), preferred_element_type=jnp.float32)


def plain_call(kernel, out_shape, in_memory, scratch=(), flops=0, num_bytes=0):
    return pl.pallas_call(
        kernel,
        out_shape=out_shape,
        in_specs=[pl.BlockSpec(memory_space=space) for space in in_memory],
        out_specs=tuple(pl.BlockSpec(memory_space=pltpu.VMEM) for _ in out_shape),
        scratch_shapes=list(scratch),
        compiler_params=pltpu.CompilerParams(vmem_limit_bytes=16 * 1024 * 1024),
        cost_estimate=pl.CostEstimate(flops=flops, bytes_accessed=num_bytes, transcendentals=0),
    )


class Sizes:
    def __init__(self, requests, steps, kv, group, levels, pages, page_tok):
        self.requests, self.steps, self.kv, self.group = requests, steps, kv, group
        self.levels, self.pages, self.page_tok = levels, pages, page_tok
        self.rows = steps * group
        self.step_rows = kv * group
        self.all_rows = requests * kv * self.rows
        self.per_tile = HD // (4 * kv)
        self.tile_count = -(-requests // self.per_tile)
        self.stat_rows = self.tile_count * self.rows
        self.factor = 1.0 / math.sqrt(HD) * math.log2(math.e)

    def tiles(self):
        for tile_at in range(self.tile_count):
            first = tile_at * self.per_tile
            yield tile_at, first, min(self.requests, first + self.per_tile)

    def spread(self, q_ref, wide):
        for step in range(self.steps):
            for head in range(self.step_rows):
                at = (step * self.step_rows + head) * self.requests
                wide[at : at + self.requests, :] = q_ref[
                    step, :, head * HD : (head + 1) * HD
                ].astype(jnp.float32)

    def pick(self, wide, request, kv_head):
        parts = []
        for step in range(self.steps):
            at = (step * self.step_rows + kv_head * self.group) * self.requests
            parts.append(wide[pl.ds(at + request, self.group, stride=self.requests), :])
        return jnp.concatenate(parts, axis=0).astype(jnp.bfloat16)

    def span(self, request, kv_head):
        at = (request * self.kv + kv_head) * self.rows
        return pl.ds(at if isinstance(at, int) else pl.multiple_of(at, 16), self.rows)

    def find(self, table_ref, count_ref, owner, request):
        slot, used = jnp.int32(0), jnp.int32(0)
        for level in range(self.levels):
            index = table_ref[level, request]
            hit = index // self.pages == owner
            slot = jnp.where(hit, index % self.pages, slot)
            used = jnp.where(hit, 1, used)
        return slot, used * count_ref[slot]


def shared_kernel(
    sz, chunk, exact, table_ref, count0_ref, count1_ref, q_ref, k0, v0, k1, v1, *rest
):
    *outs, wide = rest
    num_ref = outs[0]
    me = lax.axis_index("page")
    mate = jnp.bitwise_xor(me, 1)
    lane_ids = lax.broadcasted_iota(jnp.int32, (sz.rows, HD), 1)
    token_ids = lax.broadcasted_iota(jnp.int32, (sz.rows, sz.page_tok), 1)
    heads = range(sz.kv)
    sz.spread(q_ref, wide)
    for tile_at, first, last in sz.tiles():
        tile = jnp.zeros((sz.rows, HD), jnp.float32)
        for start in range(first, last, 8):
            items = []
            for request in range(start, min(last, start + 8)):
                slot0, count0 = sz.find(table_ref, count0_ref, me, request)
                slot1, count1 = sz.find(table_ref, count1_ref, mate, request)
                allowed = jnp.concatenate([token_ids < count0, token_ids < count1], axis=1)
                items += [(request, head, slot0, slot1, allowed) for head in heads]
            scores = []
            for request, head, slot0, slot1, allowed in items:
                cols = slice(head * HD, (head + 1) * HD)
                keys = jnp.concatenate([k0[slot0, :, cols], k1[slot1, :, cols]], 0)
                s = dot_nt(sz.pick(wide, request, head), keys)
                scores.append(jnp.where(allowed, s, NEG))
            point = [sum(two_pieces(jnp.max(s, axis=1, keepdims=True))) for s in scores]
            weights = [jnp.exp2((s - p) * sz.factor) for s, p in zip(scores, point)]
            total = [jnp.sum(w, axis=1, keepdims=True) for w in weights]
            for at, (request, head, slot0, slot1, _) in enumerate(items):
                cols = slice(head * HD, (head + 1) * HD)
                values = jnp.concatenate([v0[slot0, :, cols], v1[slot1, :, cols]], 0)
                num = dot_nn(weights[at].astype(jnp.bfloat16), values)
                num_ref[sz.span(request, head), :] = num.astype(num_ref.dtype)
                lane = ((request - first) * sz.kv + head) * 4
                tile = jnp.where(lane_ids == lane, point[at], tile)
                tile = jnp.where(lane_ids == lane + 2, total[at], tile)
        if exact:
            outs[1][pl.ds(tile_at * sz.rows, sz.rows), :] = tile
        else:
            put_stats(sz, num_ref, tile_at, tile)


def put_stats(sz, out_ref, tile_at, tile):
    kind = lax.broadcasted_iota(jnp.int32, tile.shape, 1) % 4
    high, low = two_pieces(tile)
    tile = jnp.where(kind % 2 == 0, high, pltpu.roll(low, 1, 1))
    out_ref[pl.ds(sz.all_rows + tile_at * sz.rows, sz.rows), :] = tile.astype(jnp.bfloat16)


def local_kernel(
    sz,
    chunk,
    table_ref,
    count0_ref,
    count1_ref,
    leaf_count_ref,
    q_ref,
    k0,
    v0,
    k1,
    v1,
    leaf_k_any,
    leaf_v_any,
    new_k,
    new_v,
    num_ref,
    stat_ref,
    wide,
    fresh_k,
    fresh_v,
    leaf_k,
    leaf_v,
    leaf_sem,
):
    def leaf_copy(request, whole, part, sem_at):
        return pltpu.make_async_copy(
            whole.at[chunk * sz.requests + request], part.at[request], leaf_sem.at[request, sem_at]
        )

    for request in range(sz.requests):
        leaf_copy(request, leaf_k_any, leaf_k, 0).start()
        leaf_copy(request, leaf_v_any, leaf_v, 1).start()
    me = lax.axis_index("page")
    mate = jnp.bitwise_xor(me, 1)
    lane_ids = lax.broadcasted_iota(jnp.int32, (sz.rows, HD), 1)
    token_ids = lax.broadcasted_iota(jnp.int32, (sz.rows, sz.page_tok), 1)
    fresh = fresh_k.shape[0]
    fresh_ids = lax.broadcasted_iota(jnp.int32, (sz.rows, fresh), 1)
    step_ids = lax.broadcasted_iota(jnp.int32, (sz.rows, fresh), 0) // sz.group
    device_requests = new_k.shape[1]
    causal = (fresh_ids // device_requests) <= step_ids
    fresh_request = fresh_ids % device_requests
    heads = range(sz.kv)
    cols = [slice(head * HD, (head + 1) * HD) for head in heads]
    sz.spread(q_ref, wide)
    for new_ref, full in ((new_k, fresh_k), (new_v, fresh_v)):
        rows = [new_ref[step].astype(jnp.float32) for step in range(sz.steps)]
        filler = fresh - sz.steps * device_requests
        if filler:
            rows.append(jnp.zeros((filler, sz.kv * HD), jnp.float32))
        full[...] = jnp.concatenate(rows, axis=0).astype(full.dtype)
    for tile_at, first, last in sz.tiles():
        tile = jnp.zeros((sz.rows, HD), jnp.float32)
        for start in range(first, last, 2):
            items = []
            for request in range(start, min(last, start + 2)):
                row = chunk * sz.requests + request
                slot0, count0 = sz.find(table_ref, count0_ref, me, row)
                slot1, count1 = sz.find(table_ref, count1_ref, mate, row)
                allowed = (
                    token_ids < count0,
                    token_ids < count1,
                    token_ids < leaf_count_ref[row],
                    causal & (fresh_request == row),
                )
                allowed = jnp.concatenate(allowed, axis=1)
                places = ((k0, v0, slot0), (k1, v1, slot1), (leaf_k, leaf_v, request))
                items += [(request, head, places, allowed) for head in heads]
                leaf_copy(request, leaf_k_any, leaf_k, 0).wait()
                leaf_copy(request, leaf_v_any, leaf_v, 1).wait()
            scores = []
            for request, head, places, allowed in items:
                keys = [keys[at, :, cols[head]] for keys, _, at in places]
                keys = jnp.concatenate(keys + [fresh_k[:, cols[head]]], 0)
                s = dot_nt(sz.pick(wide, request, head), keys)
                scores.append(jnp.where(allowed, s, NEG))
            top = [jnp.max(s, axis=1, keepdims=True) for s in scores]
            weights = [jnp.exp2((s - t) * sz.factor) for s, t in zip(scores, top)]
            total = [jnp.sum(w, axis=1, keepdims=True) for w in weights]
            for at, (request, head, places, _) in enumerate(items):
                values = [values[slot, :, cols[head]] for _, values, slot in places]
                values = jnp.concatenate(values + [fresh_v[:, cols[head]]], 0)
                num_ref[sz.span(request, head), :] = dot_nn(
                    weights[at].astype(jnp.bfloat16), values
                )
                lane = ((request - first) * sz.kv + head) * 4
                tile = jnp.where(lane_ids == lane, top[at], tile)
                tile = jnp.where(lane_ids == lane + 2, total[at], tile)
        stat_ref[pl.ds(tile_at * sz.rows, sz.rows), :] = tile


def merge_kernel(sz, num_ref, stat_ref, came_ref, out_ref):
    for tile_at, first, last in sz.tiles():
        came_span = pl.ds(sz.all_rows + tile_at * sz.rows, sz.rows)
        mine = stat_ref[pl.ds(tile_at * sz.rows, sz.rows), :]
        came = pair_sums(came_ref[came_span, :].astype(jnp.float32))
        top = jnp.maximum(mine, came)
        keep, add = jnp.exp2((mine - top) * sz.factor), jnp.exp2((came - top) * sz.factor)
        total = mine * pltpu.roll(keep, 2, 1) + came * pltpu.roll(add, 2, 1)
        kind = lax.broadcasted_iota(jnp.int32, top.shape, 1) % 4
        put_stats(sz, out_ref, tile_at, jnp.where(kind == 0, top, total))
        for request in range(first, last):
            for head in range(sz.kv):
                lane = ((request - first) * sz.kv + head) * 4
                span = sz.span(request, head)
                joined = num_ref[span, :] * keep[:, lane : lane + 1]
                joined = joined + came_ref[span, :].astype(jnp.float32) * add[:, lane : lane + 1]
                out_ref[span, :] = joined.astype(jnp.bfloat16)


def join_kernel(sz, num_ref, stat_ref, came_ref, out_ref, out_stat_ref):
    mine = stat_ref[...]
    came = pair_sums(came_ref[sz.all_rows : sz.all_rows + sz.rows, :].astype(jnp.float32))
    top = jnp.maximum(mine, came)
    keep, add = jnp.exp2((mine - top) * sz.factor), jnp.exp2((came - top) * sz.factor)
    total = mine * pltpu.roll(keep, 2, 1) + came * pltpu.roll(add, 2, 1)
    kind = lax.broadcasted_iota(jnp.int32, top.shape, 1) % 4
    out_stat_ref[...] = jnp.where(kind == 0, top, total)
    for request in range(sz.requests):
        for head in range(sz.kv):
            lane = (request * sz.kv + head) * 4
            span = sz.span(request, head)
            joined = num_ref[span, :] * keep[:, lane : lane + 1]
            out_ref[span, :] = joined + came_ref[span, :].astype(jnp.float32) * add[
                :, lane : lane + 1
            ]


def final_kernel(whole, sz, num_ref, stat_ref, *refs):
    *came_refs, out_ref, wide = refs
    lanes = sz.requests * sz.kv * 4
    lane_ids = lax.broadcasted_iota(jnp.int32, (sz.rows, HD), 1)
    mine = stat_ref[...]
    came = jnp.zeros((sz.rows, HD), jnp.float32)
    for chunk, came_ref in enumerate(came_refs):
        tile = pair_sums(came_ref[sz.all_rows : sz.all_rows + sz.rows, :].astype(jnp.float32))
        if chunk:
            tile = pltpu.roll(tile, chunk * lanes, 1)
        came = jnp.where(lane_ids // lanes == chunk, tile, came)
    top = jnp.maximum(mine, came)
    keep, add = jnp.exp2((mine - top) * sz.factor), jnp.exp2((came - top) * sz.factor)
    total = mine * pltpu.roll(keep, 2, 1) + came * pltpu.roll(add, 2, 1)
    total = pltpu.roll(total, HD - 2, 1)
    keep, add = keep / total, add / total
    for row in range(whole.requests):
        chunk, request = row // sz.requests, row % sz.requests
        for head in range(sz.kv):
            lane = (row * sz.kv + head) * 4
            joined = num_ref[whole.span(row, head), :] * keep[:, lane : lane + 1]
            joined = joined + came_refs[chunk][sz.span(request, head), :].astype(
                jnp.float32
            ) * add[:, lane : lane + 1]
            for step in range(sz.steps):
                at = (step * sz.step_rows + head * sz.group) * whole.requests
                wide[pl.ds(at + row, sz.group, stride=whole.requests), :] = joined[
                    step * sz.group : (step + 1) * sz.group
                ]
    for step in range(sz.steps):
        for head in range(sz.step_rows):
            at = (step * sz.step_rows + head) * whole.requests
            out_ref[step, :, head * HD : (head + 1) * HD] = wide[
                at : at + whole.requests, :
            ].astype(jnp.bfloat16)


def fetch_kernel(k_any, v_any, k_ref, v_ref, sems):
    copies = [
        pltpu.make_async_copy(source, target, sems.at[at])
        for at, (source, target) in enumerate(((k_any, k_ref), (v_any, v_ref)))
    ]
    for copy in copies:
        copy.start()
    for copy in copies:
        copy.wait()


def line_shards(
    queries,
    page_keys,
    page_values,
    page_count,
    leaf_keys,
    leaf_values,
    leaf_count,
    new_keys,
    new_values,
    path_owner,
    path_slot,
):
    requests, steps, width = queries.shape
    owners = lax.axis_size("page")
    kv = page_keys.shape[2] // HD
    pages, page_tok = page_keys.shape[:2]
    chunks = 1
    line = (queries, page_keys, page_values, page_count, leaf_keys, leaf_values, leaf_count)
    if requests % chunks or requests * kv * 4 != HD:
        return shards(*line, new_keys, new_values, path_owner, path_slot)
    shape_of = (steps, kv, QH // KVH, path_owner.shape[1], pages, page_tok)
    whole, sz = Sizes(requests, *shape_of), Sizes(requests // chunks, *shape_of)

    def exchange(array, hop):
        return lax.ppermute(array, "page", [(at, at ^ hop) for at in range(owners)])

    def after(array, *others):
        return lax.optimization_barrier((array, *others))[0]

    near, far = CORES, owners - CORES
    smem, vmem, hbm = pltpu.SMEM, pltpu.VMEM, pl.ANY
    shape = jax.ShapeDtypeStruct
    wide = pltpu.VMEM((whole.all_rows + requests, HD), jnp.float32)
    fresh_rows = -(-requests * steps // page_tok) * page_tok
    fresh = pltpu.VMEM((fresh_rows, kv * HD), jnp.bfloat16)
    leaves = pltpu.VMEM((requests, page_tok, kv * HD), jnp.bfloat16)

    def sent(size):
        return (shape((size.all_rows + size.stat_rows, HD), jnp.bfloat16),)

    def exact(size):
        return (
            shape((size.all_rows, HD), jnp.float32),
            shape((size.stat_rows, HD), jnp.float32),
        )

    block = jnp.swapaxes(queries, 0, 1)
    table = jnp.swapaxes(path_owner * pages + path_slot, 0, 1)
    far_q = exchange(block, far)
    near_q = exchange(block, near)
    mate_keys, mate_values, mate_count = (
        exchange(array, 1) for array in (page_keys, page_values, page_count)
    )
    counts = (page_count, mate_count)
    own_pages = plain_call(
        fetch_kernel,
        (shape(page_keys.shape, page_keys.dtype),) * 2,
        [hbm] * 2,
        [pltpu.SemaphoreType.DMA((2,))],
    )(after(page_keys, mate_keys, mate_values, mate_count), page_values)
    all_pages = (*own_pages, mate_keys, mate_values)
    near_table, far_table, cross_table = (exchange(table, hop) for hop in (near, far, near ^ far))
    far_q, near_table, far_table, cross_table = lax.optimization_barrier(
        (far_q, near_table, far_table, cross_table, *all_pages, mate_count)
    )[:4]

    def shared(size, chunk, is_exact, paths, rows):
        return plain_call(
            functools.partial(shared_kernel, size, chunk, is_exact),
            exact(size) if is_exact else sent(size),
            [smem] * 3 + [vmem] * 5,
            [wide],
        )(paths, *counts, rows, *all_pages)

    def merge(part, came):
        return plain_call(functools.partial(merge_kernel, sz), sent(sz), [vmem] * 3)(*part, came)[0]

    cross_q = exchange(far_q, near)
    near_q = after(near_q, far_q)
    far_part = shared(sz, 0, True, far_table, after(far_q, near_q))
    cross_q = after(cross_q, *far_part)
    cross_part = shared(sz, 0, False, cross_table, cross_q)[0]
    cross_back = exchange(cross_part, near)
    near_part = shared(sz, 0, False, near_table, after(near_q, cross_part))[0]
    cross_back = after(cross_back, near_part)
    joined = merge(far_part, cross_back)
    far_back = exchange(joined, far)
    near_back = exchange(after(near_part, joined), near)
    local = plain_call(
        functools.partial(local_kernel, whole, 0),
        exact(whole),
        [smem] * 4 + [vmem] * 5 + [hbm] * 2 + [vmem] * 2,
        [wide, fresh, fresh, leaves, leaves, pltpu.SemaphoreType.DMA((requests, 2))],
    )(
        table,
        *counts,
        leaf_count,
        after(block, joined),
        *all_pages,
        leaf_keys,
        leaf_values,
        jnp.swapaxes(new_keys, 0, 1),
        jnp.swapaxes(new_values, 0, 1),
    )
    state = plain_call(functools.partial(join_kernel, whole), exact(whole), [vmem] * 3)(
        *local, after(near_back, *local)
    )
    (out,) = plain_call(
        functools.partial(final_kernel, whole, sz),
        (shape((steps, requests, width), jnp.bfloat16),),
        [vmem] * 3,
        [wide],
    )(*state, far_back)
    return jnp.swapaxes(out, 0, 1)


def solution(mesh):
    on_line = mesh.shape["sub"] == 1 and mesh.shape["page"] == 4 * CORES
    return jax.shard_map(
        line_shards if on_line else shards,
        mesh=mesh,
        in_specs=(
            P(("groups", "page", "sub"), None, "head"),
            P(("groups", "page"), None, "head"),
            P(("groups", "page"), None, "head"),
            P(("groups", "page")),
            P(("groups", "page", "sub"), None, "head"),
            P(("groups", "page", "sub"), None, "head"),
            P(("groups", "page", "sub")),
            P(("groups", "page", "sub"), None, "head"),
            P(("groups", "page", "sub"), None, "head"),
            P(("groups", "page", "sub"), None),
            P(("groups", "page", "sub"), None),
        ),
        out_specs=P(("groups", "page", "sub"), None, "head"),
        check_vma=False,
    )
```
